256 devices in a mesh: samp: 64 (over y_lo, x, z), par: 4 (over y_hi, core).
Axes of the slice: x: 4, y: 4 (y_hi: 2, y_lo: 2; y = y_hi * 2 + y_lo), z: 8, core: 2. Of those that a mesh axis runs over, the one named last changes fastest.
Arguments:
- log_derivs: bfloat16 [8192, 8192], P('samp', 'par'), may hold values from -16 to 16
- sample_vector: float32 [8192], P('samp'), may hold values from -6 to 6
Outputs:
- gram: float32 [8192, 8192], P('samp', 'par')
- update: float32 [4, 2048], P('par', 'samp')
The draws below stay inside these ranges and needn't reach their ends.
All inputs are finite; a program needn't handle non-finite values.
Results may differ from the reference program's by a relative error of at most 0.0003.
Values may be sent and summed in bfloat16 or wider, within the bound.
No kernel may reach another device: no remote copies, remote signals or barrier semaphores. Data moves between devices by JAX's collectives and lax.ppermute only.
A program may use at most 128 MiB of HBM per device.

```python
import math
import jax
import jax.numpy as jnp
from jax import lax

PC = 2048
NS = 8192
NP = 8192
N_PAR = 4


def strengthened(entries, key, source, target, blocks, factor):
    def block_of(axis_at):
        return (jnp.arange(entries.shape[axis_at]) // (entries.shape[axis_at] // blocks)).reshape((-1,) + (1,) * (entries.ndim - 1 - axis_at))

    first = jax.random.permutation(key, blocks)[block_of(target)]
    other_side = (block_of(target) + blocks // 2) % blocks
    return jnp.where((block_of(source) == first) | (block_of(source) == other_side), factor * entries, entries)


def shard_levels(own_key, extent, pieces, least, top_value):
    level, own = 1.0, jax.random.fold_in(own_key, 6)
    for axis_at, blocks in pieces:
        steps = jnp.exp(jax.random.uniform(jax.random.fold_in(own, axis_at), (blocks,), jnp.float32, least / len(pieces), top_value / len(pieces)))
        level = level * jnp.repeat(steps, extent[axis_at] // blocks).reshape([-1 if axis == axis_at else 1 for axis in range(len(extent))])
    return level


def centred(stream_key, shape, spread, limit, shards=(), held_as=jnp.bfloat16):
    entries = spread * jax.random.normal(stream_key, shape, jnp.float32)
    if shards:
        entries = entries * shard_levels(stream_key, shape, shards, -0.22, 0.18)
    return jnp.clip(entries, -limit, limit).astype(held_as)


def bell_draw_with(stream_key, extent, width, bound, shards, heavy, dtype=jnp.bfloat16):
    drawn = width * jax.random.normal(stream_key, extent, jnp.float32)
    if shards:
        drawn = drawn * shard_levels(stream_key, extent, shards, -0.22, 0.18)
    return jnp.clip(strengthened(drawn, jax.random.fold_in(stream_key, 3), *heavy), -bound, bound).astype(dtype)


def setup_inputs(seed: int = 0) -> dict:
    keys = jax.random.split(jax.random.key(seed), 3)
    log_derivs = bell_draw_with(keys[0], (NS, NP), 1.0, 16.0, ((0, 64), (1, 4)), (0, 1, 64, 4.0))
    sample_vector = centred(keys[1], (NS,), 1.0, 6.0, ((0, 64),), jnp.float32)
    return {"log_derivs": log_derivs, "sample_vector": sample_vector}


def reference(log_derivs, sample_vector):
    total_params = log_derivs.shape[1]
    total_samples = log_derivs.shape[0]
    gram = jnp.dot(log_derivs, log_derivs.T, preferred_element_type=jnp.float32) * (1.0 / math.sqrt(total_params))
    flat = jnp.dot(sample_vector, log_derivs.astype(jnp.float32), precision=lax.Precision.HIGHEST)
    update = (flat * (1.0 / math.sqrt(total_samples))).reshape(N_PAR, PC)
    return (gram, update)
```

```python
import math

import jax
import jax.numpy as jnp
from jax import lax
from jax.experimental import pallas as pl
from jax.experimental.pallas import tpu as pltpu
from jax.sharding import Mesh, PartitionSpec as P

AXES = ("ylo", "x", "z", "yhi", "core")
SIZES = (2, 4, 8, 2, 2)
ROWS, PANEL = 128, 2048
NX, NZ = 4, 8
F32 = jnp.float32


def shift(value, axis, size, by):
    return lax.ppermute(value, axis, [(i, (i + by) % size) for i in range(size)])


def ring(own, axis, size):
    right, left = [own], [own]
    for _ in range(size // 2 - 1):
        right.append(shift(right[-1], axis, size, 1))
        left.append(shift(left[-1], axis, size, -1))
    half = own.shape[0] // 2
    first = shift(right[-1][:half], axis, size, 1)
    second = shift(left[-1][half:], axis, size, -1)
    return right, left, (first, second)


def slot_of(ylo_other, x_offset):
    x = lax.rem(lax.axis_index("x") + x_offset, NX)
    ylo = lax.rem(lax.axis_index("ylo") + ylo_other, 2)
    core = lax.rem(lax.div(x, 2) + lax.axis_index("core"), 2)
    yhi = lax.rem(ylo + lax.axis_index("yhi"), 2)
    return 2 * core + yhi, lax.rem(x, 2)


def products_kernel(scale, n_rows, n_cols, places, *refs):
    rows, cols = refs[:n_rows], refs[n_rows : n_rows + n_cols]
    keep, send, held, sems = refs[n_rows + n_cols :]
    copies = []
    for i, (ref, (ylo_other, x_offset, start)) in enumerate(zip(cols, places)):
        pair, odd = slot_of(ylo_other, x_offset)
        to = pl.multiple_of(odd * ROWS + start, 64)
        copy = pltpu.make_async_copy(ref, held.at[pair, pl.ds(to, ref.shape[0])], sems.at[i])
        copy.start()
        copies.append(copy)
    for copy in copies:
        copy.wait()
    block = jnp.concatenate([r[...] for r in rows], axis=0)
    for pair in range(4):
        out = keep if pair < 2 else send
        out[:, 256 * (pair % 2) : 256 * (pair % 2) + 256] = scale * lax.dot_general(
            block, held[pair], (((1,), (1,)), ((), ())), preferred_element_type=F32
        )


def products(scale, rows, cols, places):
    m = sum(r.shape[0] for r in rows)
    out = jax.ShapeDtypeStruct((m, 512), F32)
    vmem, anywhere = pl.BlockSpec(memory_space=pltpu.VMEM), pl.BlockSpec(memory_space=pl.ANY)

    def kernel(*refs):
        products_kernel(scale, len(rows), len(cols), places, *refs)

    return pl.pallas_call(
        kernel,
        out_shape=(out, out),
        in_specs=[vmem] * len(rows) + [anywhere] * len(cols),
        out_specs=(vmem, vmem),
        scratch_shapes=[
            pltpu.VMEM((4, 256, PANEL), jnp.bfloat16),
            pltpu.SemaphoreType.DMA((len(cols),)),
        ],
        compiler_params=pltpu.CompilerParams(vmem_limit_bytes=40 * 2**20),
        cost_estimate=pl.CostEstimate(
            flops=2 * m * 1024 * PANEL, bytes_accessed=2**22 + m * 8192, transcendentals=0
        ),
    )(*rows, *cols)


def term_kernel(places, vec, *refs):
    cols, out = refs[:-3], refs[-3]
    held, sems = refs[-2:]
    u = lax.axis_index("ylo") * NX + lax.axis_index("x")
    at = pl.multiple_of(u * 256, 256)
    copies = []
    for i, (ref, (ylo_other, x_offset, start)) in enumerate(zip(cols, places)):
        x = lax.rem(lax.axis_index("x") + x_offset, NX)
        ylo = lax.rem(lax.axis_index("ylo") + ylo_other, 2)
        to = pl.multiple_of((ylo * NX + x) * ROWS + start, 64)
        copy = pltpu.make_async_copy(
            ref.at[:, pl.ds(at, 256)], held.at[pl.ds(to, ref.shape[0])], sems.at[i]
        )
        copy.start()
        copies.append(copy)
    for copy in copies:
        copy.wait()
    v = vec[...]
    total = jnp.zeros((8, 256), F32)
    for _ in range(3):
        part = v.astype(jnp.bfloat16)
        v = v - part.astype(F32)
        total += jnp.dot(part, held[...], preferred_element_type=F32)
    out[...] = total


def term(vec, cols, places):
    vmem, anywhere = pl.BlockSpec(memory_space=pltpu.VMEM), pl.BlockSpec(memory_space=pl.ANY)

    def kernel(*refs):
        term_kernel(places, *refs)

    return pl.pallas_call(
        kernel,
        out_shape=jax.ShapeDtypeStruct((8, 256), F32),
        in_specs=[vmem] + [anywhere] * len(cols),
        out_specs=vmem,
        scratch_shapes=[
            pltpu.VMEM((1024, 256), jnp.bfloat16),
            pltpu.SemaphoreType.DMA((len(cols),)),
        ],
        cost_estimate=pl.CostEstimate(flops=2**23, bytes_accessed=2**19, transcendentals=0),
    )(vec, *cols)


def place_kernel(offsets, *refs):
    blocks, out = refs[:-1], refs[-1]
    for block, offset in zip(blocks, offsets):
        z = lax.rem(lax.axis_index("z") + offset, NZ)
        at = pl.multiple_of(z * ROWS, ROWS)
        out[:, pl.ds(at, ROWS)] = block[:, :ROWS]
        out[:, pl.ds(at + NZ * ROWS, ROWS)] = block[:, ROWS:]


def place(blocks, offsets):
    vmem = pl.BlockSpec(memory_space=pltpu.VMEM)

    def kernel(*refs):
        place_kernel(offsets, *refs)

    return pl.pallas_call(
        kernel,
        out_shape=jax.ShapeDtypeStruct((ROWS, PANEL), F32),
        in_specs=[vmem] * len(blocks),
        out_specs=vmem,
        cost_estimate=pl.CostEstimate(flops=0, bytes_accessed=2**21, transcendentals=0),
    )(*blocks)


def body(log_derivs, sample_vector):
    scale_gram = 1.0 / math.sqrt(PANEL * 4)
    scale_update = 1.0 / math.sqrt(ROWS * 64)

    vec = lax.all_gather(sample_vector, ("ylo", "x"), axis=0, tiled=True)

    z_right, z_left, z_far = ring(log_derivs, "z", NZ)
    partner = shift(log_derivs, "ylo", 2, 1)
    cols, places = [], []
    for ylo_other, own in ((0, log_derivs), (1, partner)):
        right, left, far = ring(own, "x", NX)
        cols += [own, right[1], left[1], *far]
        places += [(ylo_other, 0, 0), (ylo_other, 3, 0), (ylo_other, 1, 0), (ylo_other, 2, 0), (ylo_other, 2, 64)]

    mine = jnp.sum(term(jnp.broadcast_to(vec[None], (8, 1024)), cols, places)[:1], axis=0)
    shared = lax.all_gather(mine[None], "z", axis=0, tiled=True)
    owned = lax.dynamic_slice_in_dim(jnp.sum(shared, axis=0), lax.axis_index("z") * 32, 32)
    update = (owned * scale_update)[None]

    groups = [
        ([0, 1, -1], [log_derivs, z_right[1], z_left[1]]),
        ([2, -2], [z_right[2], z_left[2]]),
        ([3, -3, 4], [z_right[3], z_left[3], *z_far]),
    ]
    blocks, offsets = [], []
    for backs, rows in groups:
        keep, send = products(scale_gram, rows, cols, places)
        both = keep + shift(send, "core", 2, 1)
        full = both[:, :256] + shift(both[:, 256:], "yhi", 2, 1)
        for i, back in enumerate(backs):
            block = full[ROWS * i : ROWS * (i + 1)]
            blocks.append(block if back == 0 else shift(block, "z", NZ, -back))
            offsets.append(back % NZ)
    return place(blocks, offsets), update


def solution(mesh):
    fine = Mesh(mesh.devices.reshape(SIZES), AXES)
    samp, par = AXES[:3], AXES[3:]
    return jax.shard_map(
        body,
        mesh=fine,
        in_specs=(P(samp, par), P(samp)),
        out_specs=(P(samp, par), P(par, samp)),
        check_vma=False,
    )
```

```python
import math

import jax
import jax.numpy as jnp
from jax import lax
from jax.experimental import pallas as pl
from jax.experimental.pallas import tpu as pltpu
from jax.sharding import Mesh, PartitionSpec as P

AXES = ("ylo", "x", "z", "yhi", "core")
SIZES = (2, 4, 8, 2, 2)
ROWS, PANEL = 128, 2048
NX, NZ = 4, 8
F32 = jnp.float32
GROUPS = ((0, 1, -1), (2, -2, 3, -3, 4))
VMEM = pl.BlockSpec(memory_space=pltpu.VMEM)
ANYWHERE = pl.BlockSpec(memory_space=pl.ANY)
SMALL = pltpu.CompilerParams(vmem_limit_bytes=16 * 2**20)


def shift(value, axis, by):
    size = SIZES[AXES.index(axis)]
    pairs = [(2 * i + c, 2 * ((i + (by, -by)[c]) % size) + c) for i in range(size) for c in range(2)]
    return lax.ppermute(value, (axis, "core"), pairs)


def swap(value, axis):
    return lax.ppermute(value, axis, [(0, 1), (1, 0)])


def turn(by):
    return by * (1 - 2 * lax.axis_index("core"))


def after(value, *others):
    return lax.optimization_barrier((value, *others))[0]


def gather(log_derivs, packed):
    rows = {0: log_derivs}
    rows[1], rows[-1] = shift(log_derivs, "z", 1), shift(log_derivs, "z", -1)
    partner = swap(packed, "ylo")
    columns = {(0, 0): packed, (1, 0): partner}
    for by in (1, -1):
        columns[0, by] = shift(packed, "x", by)
    rows[2], rows[-2] = shift(rows[1], "z", 1), shift(rows[-1], "z", -1)
    for by in (1, -1):
        columns[1, by] = shift(partner, "x", by)
    rows[3], rows[-3] = shift(rows[2], "z", 1), shift(rows[-2], "z", -1)
    columns[0, 2] = shift(columns[0, 1], "x", 1)
    columns[1, 2] = shift(columns[1, 1], "x", 1)
    rows[4] = shift(rows[3], "z", 1)
    return rows, columns


def pack(log_derivs, sample_vector):
    def kernel(entries, vec, out):
        out[:, :PANEL] = entries[...]
        left = jnp.transpose(jnp.broadcast_to(vec[...], (ROWS, ROWS)))
        lane = lax.broadcasted_iota(jnp.int32, (ROWS, ROWS), 1)
        parts = jnp.zeros((ROWS, ROWS), F32)
        for i in range(3):
            part = left.astype(jnp.bfloat16).astype(F32)
            left = left - part
            parts = jnp.where(lane == i, part, parts)
        out[:, PANEL:] = parts.astype(jnp.bfloat16)

    return pl.pallas_call(
        kernel,
        out_shape=jax.ShapeDtypeStruct((ROWS, PANEL + ROWS), jnp.bfloat16),
        in_specs=[VMEM] * 2,
        out_specs=VMEM,
        compiler_params=SMALL,
        cost_estimate=pl.CostEstimate(flops=0, bytes_accessed=2**20, transcendentals=0),
    )(log_derivs, sample_vector[None])


def products(scale, rows, columns):
    m, n = ROWS * len(rows), len(rows)

    def kernel(*refs):
        cols = refs[n : n + len(columns)]
        keep, send, held, sems = refs[n + len(columns) :]
        copies = []
        for i, (ref, (ylo, back)) in enumerate(zip(cols, columns)):
            x = lax.rem(lax.axis_index("x") + NX - turn(back), NX)
            core = lax.rem(lax.div(x, 2) + lax.axis_index("core"), 2)
            yhi = lax.rem(lax.axis_index("ylo") + ylo + lax.axis_index("yhi"), 2)
            to = pl.multiple_of(lax.rem(x, 2) * ROWS, ROWS)
            copy = pltpu.make_async_copy(
                ref.at[:, pl.ds(0, PANEL)], held.at[2 * core + yhi, pl.ds(to, ROWS)], sems.at[i]
            )
            copy.start()
            copies.append(copy)
        for copy in copies:
            copy.wait()
        block = jnp.concatenate([r[...] for r in refs[:n]], axis=0)
        for pair in range(4):
            out = keep if pair < 2 else send
            out[:, 256 * (pair % 2) : 256 * (pair % 2) + 256] = scale * lax.dot_general(
                block, held[pair], (((1,), (1,)), ((), ())), preferred_element_type=F32
            )

    out = jax.ShapeDtypeStruct((m, 512), F32)
    return pl.pallas_call(
        kernel,
        out_shape=(out, out),
        in_specs=[VMEM] * n + [ANYWHERE] * len(columns),
        out_specs=(VMEM, VMEM),
        scratch_shapes=[
            pltpu.VMEM((4, 256, PANEL), jnp.bfloat16),
            pltpu.SemaphoreType.DMA((len(columns),)),
        ],
        compiler_params=pltpu.CompilerParams(vmem_limit_bytes=24 * 2**20),
        cost_estimate=pl.CostEstimate(
            flops=2 * m * 1024 * PANEL, bytes_accessed=2**22 + m * 8192, transcendentals=0
        ),
    )(*rows, *columns.values())


def term(scale, columns):
    def kernel(*refs):
        cols = refs[: len(columns)]
        out, held, vecs, sems = refs[len(columns) :]
        u = lax.axis_index("ylo") * NX + lax.axis_index("x")
        mine = pl.multiple_of(u * 256, 256)
        copies = []
        for i, ref in enumerate(cols):
            for j, (part, target) in enumerate(((pl.ds(mine, 256), held), (pl.ds(PANEL, ROWS), vecs))):
                copy = pltpu.make_async_copy(
                    ref.at[:, part], target.at[pl.ds(ROWS * i, ROWS)], sems.at[2 * i + j]
                )
                copy.start()
                copies.append(copy)
        for copy in copies:
            copy.wait()
        parts = lax.dot_general(
            vecs[...], held[...], (((0,), (0,)), ((), ())), preferred_element_type=F32
        )
        out[...] = jnp.broadcast_to(scale * jnp.sum(parts, axis=0, keepdims=True), (8, 256))

    return pl.pallas_call(
        kernel,
        out_shape=jax.ShapeDtypeStruct((8, 256), F32),
        in_specs=[ANYWHERE] * len(columns),
        out_specs=VMEM,
        scratch_shapes=[
            pltpu.VMEM((8 * ROWS, 256), jnp.bfloat16),
            pltpu.VMEM((8 * ROWS, ROWS), jnp.bfloat16),
            pltpu.SemaphoreType.DMA((2 * len(columns),)),
        ],
        compiler_params=SMALL,
        cost_estimate=pl.CostEstimate(flops=2**26, bytes_accessed=2**20, transcendentals=0),
    )(*columns.values())


def peak(value):
    top = jnp.maximum(jnp.max(jnp.abs(value)), 1e-30)
    return jnp.broadcast_to(top, (16, 256)).astype(jnp.bfloat16)


def encode(value, top):
    power = value * (2.0**15 / top.astype(F32)[:1])
    for _ in range(3):
        power = power * power
    return jnp.where(value < 0, -power, power).astype(jnp.bfloat16)


def decode(code, top):
    code = code.astype(F32)
    root = jnp.abs(code)
    for _ in range(3):
        root = jnp.sqrt(root)
    return jnp.where(code < 0, -root, root) * (top.astype(F32)[:1] * 2.0**-15)


def split_yhi(keep, received, backs):
    m = keep.shape[0]
    order = [backs.index(-back if -back in backs else back) for back in backs]

    def kernel(a, b, own, code):
        b = jnp.concatenate([b[ROWS * i : ROWS * (i + 1)] for i in order], axis=0)
        own[...] = a[:, :256] + b[:, :256]
        other = a[:, 256:] + b[:, 256:]
        top = peak(other)
        code[:m] = encode(other, top)
        code[m:] = top

    return pl.pallas_call(
        kernel,
        out_shape=(
            jax.ShapeDtypeStruct((m, 256), F32),
            jax.ShapeDtypeStruct((m + 16, 256), jnp.bfloat16),
        ),
        in_specs=[VMEM] * 2,
        out_specs=(VMEM, VMEM),
        compiler_params=SMALL,
        cost_estimate=pl.CostEstimate(flops=0, bytes_accessed=m * 6000, transcendentals=0),
    )(keep, received)


def split_z(own, received, last_rows, backs):
    m = own.shape[0]

    def kernel(own, code, rows, *outs):
        full = own[...] + decode(code[:m], code[m:])
        left, parts = rows[:1], []
        for _ in range(3):
            parts.append(left.astype(jnp.bfloat16).astype(F32))
            left = left - parts[-1]
        row = lax.broadcasted_iota(jnp.int32, (16, 256), 0)
        for i, (back, out) in enumerate(zip(backs, outs)):
            block = full[ROWS * i : ROWS * (i + 1)]
            if back == 0:
                out[...] = block
                continue
            top = peak(block)
            out[:ROWS] = encode(block, top)
            tail = jnp.where(row == 0, top.astype(F32), 0.0)
            for j in range(3):
                tail = jnp.where(row == j + 1, parts[j], tail)
            out[ROWS:] = tail.astype(jnp.bfloat16)

    whole = jax.ShapeDtypeStruct((ROWS, 256), F32)
    coded = jax.ShapeDtypeStruct((ROWS + 16, 256), jnp.bfloat16)
    return pl.pallas_call(
        kernel,
        out_shape=tuple(coded if back else whole for back in backs),
        in_specs=[VMEM] * 3,
        out_specs=tuple(VMEM for _ in backs),
        compiler_params=SMALL,
        cost_estimate=pl.CostEstimate(flops=0, bytes_accessed=m * 2000, transcendentals=0),
    )(own, received, last_rows)


def place(blocks, backs, last_rows):
    def kernel(*refs):
        rows, out, update = refs[len(blocks) :]
        total = rows[:1]
        for block, back in zip(refs, backs):
            z = lax.rem(lax.axis_index("z") + NZ + turn(back), NZ)
            at = pl.multiple_of(z * ROWS, ROWS)
            if back:
                tail = block[ROWS:]
                value = decode(block[:ROWS], tail)
                total = total + jnp.sum(tail[1:4].astype(F32), axis=0, keepdims=True)
            else:
                value = block[...]
            out[:, pl.ds(at, ROWS)] = value[:, :ROWS]
            out[:, pl.ds(at + NZ * ROWS, ROWS)] = value[:, ROWS:]
        owned = jnp.zeros((1, 32), F32)
        for z in range(NZ):
            owned = jnp.where(lax.axis_index("z") == z, total[:, 32 * z : 32 * z + 32], owned)
        update[...] = owned

    return pl.pallas_call(
        kernel,
        out_shape=(
            jax.ShapeDtypeStruct((ROWS, PANEL), F32),
            jax.ShapeDtypeStruct((1, 32), F32),
        ),
        in_specs=[VMEM] * (len(blocks) + 1),
        out_specs=(VMEM, VMEM),
        compiler_params=SMALL,
        cost_estimate=pl.CostEstimate(flops=0, bytes_accessed=2**21, transcendentals=0),
    )(*blocks, last_rows)


def body(log_derivs, sample_vector):
    scale_gram = 1.0 / math.sqrt(PANEL * 4)
    scale_update = 1.0 / math.sqrt(ROWS * 64)

    rows, columns = gather(log_derivs, pack(log_derivs, sample_vector))
    last_rows = term(scale_update, columns)

    blocks = {}
    for backs in GROUPS:
        keep, send = products(scale_gram, [rows[back] for back in backs], columns)
        own, code = split_yhi(keep, swap(send, "core"), backs)
        for back, block in zip(backs, split_z(own, swap(code, "yhi"), last_rows, backs)):
            blocks[back] = shift(block, "z", -back) if back else block
    return place(blocks.values(), list(blocks), last_rows)


def solution(mesh):
    fine = Mesh(mesh.devices.reshape(SIZES), AXES)
    samp, par = AXES[:3], AXES[3:]
    return jax.shard_map(
        body,
        mesh=fine,
        in_specs=(P(samp, par), P(samp)),
        out_specs=(P(samp, par), P(par, samp)),
        check_vma=False,
    )
```

```python
import math

import jax
import jax.numpy as jnp
from jax import lax
from jax.experimental import pallas as pl
from jax.experimental.pallas import tpu as pltpu
from jax.sharding import Mesh, PartitionSpec as P

AXES = ("ylo", "x", "z", "yhi", "core")
SIZES = (2, 4, 8, 2, 2)
ROWS, PANEL = 128, 2048
NX, NZ = 4, 8
F32 = jnp.float32
GROUPS = ((0, 1, -1, 2, -2), (3, -3, 4))
VMEM = pl.BlockSpec(memory_space=pltpu.VMEM)
ANYWHERE = pl.BlockSpec(memory_space=pl.ANY)
SMALL = pltpu.CompilerParams(vmem_limit_bytes=16 * 2**20)


def shift(value, axis, by):
    size = SIZES[AXES.index(axis)]
    pairs = [(2 * i + c, 2 * ((i + (by, -by)[c]) % size) + c) for i in range(size) for c in range(2)]
    return lax.ppermute(value, (axis, "core"), pairs)


def swap(value, axis):
    return lax.ppermute(value, axis, [(0, 1), (1, 0)])


def turn(by):
    return by * (1 - 2 * lax.axis_index("core"))


def after(value, *others):
    return lax.optimization_barrier((value, *others))[0]


def gather(log_derivs, packed):
    z_a1, z_b1 = shift(log_derivs, "z", 1), shift(log_derivs, "z", -1)
    x_a0, x_b0 = shift(packed, "x", 1), shift(packed, "x", -1)
    partner = swap(packed, "ylo")

    z_a2, z_b2 = shift(z_a1, "z", 1), shift(z_b1, "z", -1)
    x_a1, x_far0 = shift(partner, "x", 1), shift(x_a0, "x", 1)
    x_b1 = swap(x_b0, "ylo")

    z_a3, z_b3 = shift(z_a2, "z", 1), shift(z_b2, "z", -1)
    x_far1 = shift(after(x_a1, x_far0, x_b1), "x", 1)

    z_a4 = shift(after(z_a3, z_b3), "z", 1)
    rows = {0: log_derivs, 1: z_a1, -1: z_b1, 2: z_a2, -2: z_b2, 3: z_a3, -3: z_b3, 4: z_a4}
    columns = {(0, 0): packed, (0, 1): x_a0, (0, -1): x_b0, (0, 2): x_far0}
    columns |= {(1, 0): partner, (1, 1): x_a1, (1, -1): x_b1, (1, 2): x_far1}
    return rows, columns


def pack(log_derivs, sample_vector):
    def kernel(entries, vec, out):
        out[:, :PANEL] = entries[...]
        left = jnp.transpose(jnp.broadcast_to(vec[...], (ROWS, ROWS)))
        lane = lax.broadcasted_iota(jnp.int32, (ROWS, ROWS), 1)
        parts = jnp.zeros((ROWS, ROWS), F32)
        for i in range(3):
            part = left.astype(jnp.bfloat16).astype(F32)
            left = left - part
            parts = jnp.where(lane == i, part, parts)
        out[:, PANEL:] = parts.astype(jnp.bfloat16)

    return pl.pallas_call(
        kernel,
        out_shape=jax.ShapeDtypeStruct((ROWS, PANEL + ROWS), jnp.bfloat16),
        in_specs=[VMEM] * 2,
        out_specs=VMEM,
        compiler_params=SMALL,
        cost_estimate=pl.CostEstimate(flops=0, bytes_accessed=2**20, transcendentals=0),
    )(log_derivs, sample_vector[None])


def products(scale, rows, columns):
    m, n = ROWS * len(rows), len(rows)

    def kernel(*refs):
        cols = refs[n : n + len(columns)]
        keep, *sends = refs[n + len(columns) : 2 * n + len(columns) + 1]
        held, sems = refs[2 * n + len(columns) + 1 :]
        copies = []
        for i, (ref, (ylo, back)) in enumerate(zip(cols, columns)):
            x = lax.rem(lax.axis_index("x") + NX - turn(back), NX)
            core = lax.rem(lax.div(x, 2) + lax.axis_index("core"), 2)
            yhi = lax.rem(lax.axis_index("ylo") + ylo + lax.axis_index("yhi"), 2)
            to = pl.multiple_of(lax.rem(x, 2) * ROWS, ROWS)
            copy = pltpu.make_async_copy(
                ref.at[:, pl.ds(0, PANEL)], held.at[2 * core + yhi, pl.ds(to, ROWS)], sems.at[i]
            )
            copy.start()
            copies.append(copy)
        for copy in copies:
            copy.wait()
        block = jnp.concatenate([r[...] for r in refs[:n]], axis=0)
        for pair in (2, 3, 0, 1):
            at = slice(256 * (pair % 2), 256 * (pair % 2) + 256)
            value = scale * lax.dot_general(
                block, held[pair], (((1,), (1,)), ((), ())), preferred_element_type=F32
            )
            if pair < 2:
                keep[:, at] = value
            else:
                for i, send in enumerate(sends):
                    send[:, at] = value[ROWS * i : ROWS * (i + 1)]

    out = [jax.ShapeDtypeStruct((rows, 512), F32) for rows in [m] + [ROWS] * n]
    return pl.pallas_call(
        kernel,
        out_shape=out,
        in_specs=[VMEM] * n + [ANYWHERE] * len(columns),
        out_specs=[VMEM] * (n + 1),
        scratch_shapes=[
            pltpu.VMEM((4, 256, PANEL), jnp.bfloat16),
            pltpu.SemaphoreType.DMA((len(columns),)),
        ],
        compiler_params=pltpu.CompilerParams(vmem_limit_bytes=24 * 2**20),
        cost_estimate=pl.CostEstimate(
            flops=2 * m * 1024 * PANEL, bytes_accessed=2**22 + m * 8192, transcendentals=0
        ),
    )(*rows, *columns.values())


def term(scale, columns):
    def kernel(*refs):
        cols = refs[: len(columns)]
        out, held, vecs, sems = refs[len(columns) :]
        u = lax.axis_index("ylo") * NX + lax.axis_index("x")
        mine = pl.multiple_of(u * 256, 256)
        copies = []
        for i, ref in enumerate(cols):
            for j, (part, target) in enumerate(((pl.ds(mine, 256), held), (pl.ds(PANEL, ROWS), vecs))):
                copy = pltpu.make_async_copy(
                    ref.at[:, part], target.at[pl.ds(ROWS * i, ROWS)], sems.at[2 * i + j]
                )
                copy.start()
                copies.append(copy)
        for copy in copies:
            copy.wait()
        parts = lax.dot_general(
            vecs[...], held[...], (((0,), (0,)), ((), ())), preferred_element_type=F32
        )
        out[...] = jnp.broadcast_to(scale * jnp.sum(parts, axis=0, keepdims=True), (8, 256))

    return pl.pallas_call(
        kernel,
        out_shape=jax.ShapeDtypeStruct((8, 256), F32),
        in_specs=[ANYWHERE] * len(columns),
        out_specs=VMEM,
        scratch_shapes=[
            pltpu.VMEM((8 * ROWS, 256), jnp.bfloat16),
            pltpu.VMEM((8 * ROWS, ROWS), jnp.bfloat16),
            pltpu.SemaphoreType.DMA((2 * len(columns),)),
        ],
        compiler_params=SMALL,
        cost_estimate=pl.CostEstimate(flops=2**26, bytes_accessed=2**20, transcendentals=0),
    )(*columns.values())


def peak(value):
    top = jnp.maximum(jnp.max(jnp.abs(value)), 1e-30)
    return jnp.broadcast_to(top, (16, 256)).astype(jnp.bfloat16)


def encode(value, top):
    size = jnp.log2(jnp.maximum(jnp.abs(value) * (1.0 / top.astype(F32)[:1]), 2.0**-26))
    power = jnp.exp2(jnp.maximum(126.0 + 22.0 * size, 5.0 * size - 10.0))
    return jnp.where(value < 0, -power, power).astype(jnp.bfloat16)


def decode(code, top):
    code = code.astype(F32)
    size = jnp.log2(jnp.maximum(jnp.abs(code), 2.0**-126))
    value = jnp.exp2(jnp.minimum((size - 126.0) * (1.0 / 22.0), (size + 10.0) * 0.2)) * top.astype(F32)[:1]
    return jnp.where(code < 0, -value, jnp.where(code > 0, value, 0.0))


def split_yhi(keep, received, backs):
    m = keep.shape[0]
    order = [backs.index(-back if -back in backs else back) for back in backs]

    def kernel(a, *refs):
        own, code = refs[len(backs) :]
        b = jnp.concatenate([refs[i][...] for i in order], axis=0)
        own[...] = a[:, :256] + b[:, :256]
        other = a[:, 256:] + b[:, 256:]
        top = peak(other)
        code[:m] = encode(other, top)
        code[m:] = top

    return pl.pallas_call(
        kernel,
        out_shape=(
            jax.ShapeDtypeStruct((m, 256), F32),
            jax.ShapeDtypeStruct((m + 16, 256), jnp.bfloat16),
        ),
        in_specs=[VMEM] * (1 + len(backs)),
        out_specs=(VMEM, VMEM),
        compiler_params=SMALL,
        cost_estimate=pl.CostEstimate(flops=0, bytes_accessed=m * 6000, transcendentals=0),
    )(keep, *received)


def split_z(own, received, last_rows, backs):
    m = own.shape[0]

    def kernel(own, code, rows, *outs):
        full = own[...] + decode(code[:m], code[m:])
        left, parts = rows[:1], []
        for _ in range(3):
            parts.append(left.astype(jnp.bfloat16).astype(F32))
            left = left - parts[-1]
        row = lax.broadcasted_iota(jnp.int32, (16, 256), 0)
        for i, (back, out) in enumerate(zip(backs, outs)):
            block = full[ROWS * i : ROWS * (i + 1)]
            if back == 0:
                out[...] = block
                continue
            top = peak(block)
            out[:ROWS] = encode(block, top)
            tail = jnp.where(row == 0, top.astype(F32), 0.0)
            for j in range(3):
                tail = jnp.where(row == j + 1, parts[j], tail)
            out[ROWS:] = tail.astype(jnp.bfloat16)

    whole = jax.ShapeDtypeStruct((ROWS, 256), F32)
    coded = jax.ShapeDtypeStruct((ROWS + 16, 256), jnp.bfloat16)
    return pl.pallas_call(
        kernel,
        out_shape=tuple(coded if back else whole for back in backs),
        in_specs=[VMEM] * 3,
        out_specs=tuple(VMEM for _ in backs),
        compiler_params=SMALL,
        cost_estimate=pl.CostEstimate(flops=0, bytes_accessed=m * 2000, transcendentals=0),
    )(own, received, last_rows)


def place(blocks, backs, last_rows):
    def kernel(*refs):
        rows, out, update = refs[len(blocks) :]
        total = rows[:1]
        for block, back in zip(refs, backs):
            z = lax.rem(lax.axis_index("z") + NZ + turn(back), NZ)
            at = pl.multiple_of(z * ROWS, ROWS)
            if back:
                tail = block[ROWS:]
                value = decode(block[:ROWS], tail)
                total = total + jnp.sum(tail[1:4].astype(F32), axis=0, keepdims=True)
            else:
                value = block[...]
            out[:, pl.ds(at, ROWS)] = value[:, :ROWS]
            out[:, pl.ds(at + NZ * ROWS, ROWS)] = value[:, ROWS:]
        owned = jnp.zeros((1, 32), F32)
        for z in range(NZ):
            owned = jnp.where(lax.axis_index("z") == z, total[:, 32 * z : 32 * z + 32], owned)
        update[...] = owned

    return pl.pallas_call(
        kernel,
        out_shape=(
            jax.ShapeDtypeStruct((ROWS, PANEL), F32),
            jax.ShapeDtypeStruct((1, 32), F32),
        ),
        in_specs=[VMEM] * (len(blocks) + 1),
        out_specs=(VMEM, VMEM),
        compiler_params=SMALL,
        cost_estimate=pl.CostEstimate(flops=0, bytes_accessed=2**21, transcendentals=0),
    )(*blocks, last_rows)


def body(log_derivs, sample_vector):
    scale_gram = 1.0 / math.sqrt(PANEL * 4)
    scale_update = 1.0 / math.sqrt(ROWS * 64)

    rows, columns = gather(log_derivs, pack(log_derivs, sample_vector))
    last_rows = term(scale_update, columns)

    blocks, sent, received = {}, [], []
    for backs in GROUPS:
        keep, *sends = products(scale_gram, [rows[back] for back in backs], columns)
        sends = [swap(send, "core") for send in sends]
        own, code = split_yhi(keep, sends, backs)
        code = swap(after(code, *received), "yhi")
        received.append(code)
        waited, sent = sent, []
        for back, block in zip(backs, split_z(own, code, last_rows, backs)):
            blocks[back] = shift(after(block, *waited), "z", -back) if back else block
            if back and len(sent) < 1:
                sent.append(blocks[back])
    return place(blocks.values(), list(blocks), last_rows)


def solution(mesh):
    fine = Mesh(mesh.devices.reshape(SIZES), AXES)
    samp, par = AXES[:3], AXES[3:]
    return jax.shard_map(
        body,
        mesh=fine,
        in_specs=(P(samp, par), P(samp)),
        out_specs=(P(samp, par), P(par, samp)),
        check_vma=False,
    )
```

```python
import math

import jax
import jax.numpy as jnp
from jax import lax
from jax.experimental import pallas as pl
from jax.experimental.pallas import tpu as pltpu
from jax.sharding import Mesh, PartitionSpec as P

AXES = ("ylo", "x", "z", "yhi", "core")
SIZES = (2, 4, 8, 2, 2)
ROWS, PANEL = 128, 2048
NX, NZ = 4, 8
F32 = jnp.float32
GROUPS = ((0, 1, -1, 2, -2), (3, -3, 4))
PARTS = ((160,) * 4, (128,) * 3)
COSTS = ((0, 0, 10), (2.2, 0.5, 0.5))
VMEM = pl.BlockSpec(memory_space=pltpu.VMEM)
ANYWHERE = pl.BlockSpec(memory_space=pl.ANY)
SMALL = pltpu.CompilerParams(vmem_limit_bytes=16 * 2**20)


def takes(work):
    return pl.CostEstimate(flops=int(1e9 * work), bytes_accessed=0, transcendentals=0)


def shift(value, axis, by):
    size = SIZES[AXES.index(axis)]
    pairs = [(2 * i + c, 2 * ((i + (by, -by)[c]) % size) + c) for i in range(size) for c in range(2)]
    return lax.ppermute(value, (axis, "core"), pairs)


def swap(value, axis):
    return lax.ppermute(value, axis, [(0, 1), (1, 0)])


def turn(by):
    return by * (1 - 2 * lax.axis_index("core"))


def after(value, *others):
    return lax.optimization_barrier((value, *others))[0]


def gather(log_derivs, packed):
    z_a1, z_b1 = shift(log_derivs, "z", 1), shift(log_derivs, "z", -1)
    x_a0, x_b0 = shift(packed, "x", 1), shift(packed, "x", -1)
    partner = swap(packed, "ylo")

    z_a2, z_b2 = shift(z_a1, "z", 1), shift(z_b1, "z", -1)
    x_a1, x_far0 = shift(partner, "x", 1), shift(x_a0, "x", 1)
    x_b1 = swap(x_b0, "ylo")

    z_a3, z_b3 = shift(z_a2, "z", 1), shift(z_b2, "z", -1)
    x_far1 = shift(after(x_a1, x_far0, x_b1), "x", 1)

    z_a4 = shift(after(z_a3, z_b3), "z", 1)
    rows = {0: log_derivs, 1: z_a1, -1: z_b1, 2: z_a2, -2: z_b2, 3: z_a3, -3: z_b3, 4: z_a4}
    columns = {(0, 0): packed, (0, 1): x_a0, (0, -1): x_b0, (0, 2): x_far0}
    columns |= {(1, 0): partner, (1, 1): x_a1, (1, -1): x_b1, (1, 2): x_far1}
    return rows, columns


def pack(log_derivs, sample_vector):
    def kernel(entries, vec, out):
        out[:, :PANEL] = entries[...]
        left = jnp.transpose(jnp.broadcast_to(vec[...], (ROWS, ROWS)))
        lane = lax.broadcasted_iota(jnp.int32, (ROWS, ROWS), 1)
        parts = jnp.zeros((ROWS, ROWS), F32)
        for i in range(3):
            part = left.astype(jnp.bfloat16).astype(F32)
            left = left - part
            parts = jnp.where(lane == i, part, parts)
        out[:, PANEL:] = parts.astype(jnp.bfloat16)

    return pl.pallas_call(
        kernel,
        out_shape=jax.ShapeDtypeStruct((ROWS, PANEL + ROWS), jnp.bfloat16),
        in_specs=[VMEM] * 2,
        out_specs=VMEM,
        compiler_params=SMALL,
        cost_estimate=takes(0),
    )(log_derivs, sample_vector[None])


def products(scale, rows, columns, parts, cost):
    m, n = ROWS * len(rows), len(rows)

    def kernel(*refs):
        cols = refs[n : n + len(columns)]
        keep, *sends = refs[n + len(columns) : -2]
        held, sems = refs[-2:]
        copies = []
        for i, (ref, (ylo, back)) in enumerate(zip(cols, columns)):
            x = lax.rem(lax.axis_index("x") + NX - turn(back), NX)
            core = lax.rem(lax.div(x, 2) + lax.axis_index("core"), 2)
            yhi = lax.rem(lax.axis_index("ylo") + ylo + lax.axis_index("yhi"), 2)
            to = pl.multiple_of(lax.rem(x, 2) * ROWS, ROWS)
            copy = pltpu.make_async_copy(
                ref.at[:, pl.ds(0, PANEL)], held.at[2 * core + yhi, pl.ds(to, ROWS)], sems.at[i]
            )
            copy.start()
            copies.append(copy)
        for copy in copies:
            copy.wait()
        block = jnp.concatenate([r[...] for r in refs[:n]], axis=0)
        for pair in (2, 3, 0, 1):
            at = slice(256 * (pair % 2), 256 * (pair % 2) + 256)
            value = scale * lax.dot_general(
                block, held[pair], (((1,), (1,)), ((), ())), preferred_element_type=F32
            )
            if pair < 2:
                keep[:, at] = value
            else:
                first = 0
                for send in sends:
                    send[:, at] = value[first : first + send.shape[0]]
                    first += send.shape[0]

    out = [jax.ShapeDtypeStruct((count, 512), F32) for count in (m, *parts)]
    return pl.pallas_call(
        kernel,
        out_shape=out,
        in_specs=[VMEM] * n + [ANYWHERE] * len(columns),
        out_specs=[VMEM] * len(out),
        scratch_shapes=[
            pltpu.VMEM((4, 256, PANEL), jnp.bfloat16),
            pltpu.SemaphoreType.DMA((len(columns),)),
        ],
        compiler_params=pltpu.CompilerParams(vmem_limit_bytes=24 * 2**20),
        cost_estimate=takes(cost),
    )(*rows, *columns.values())


def term(scale, columns):
    def kernel(*refs):
        cols = refs[: len(columns)]
        out, held, vecs, sems = refs[len(columns) :]
        u = lax.axis_index("ylo") * NX + lax.axis_index("x")
        mine = pl.multiple_of(u * 256, 256)
        copies = []
        for i, ref in enumerate(cols):
            for j, (part, target) in enumerate(((pl.ds(mine, 256), held), (pl.ds(PANEL, ROWS), vecs))):
                copy = pltpu.make_async_copy(
                    ref.at[:, part], target.at[pl.ds(ROWS * i, ROWS)], sems.at[2 * i + j]
                )
                copy.start()
                copies.append(copy)
        for copy in copies:
            copy.wait()
        parts = lax.dot_general(
            vecs[...], held[...], (((0,), (0,)), ((), ())), preferred_element_type=F32
        )
        out[...] = jnp.broadcast_to(scale * jnp.sum(parts, axis=0, keepdims=True), (8, 256))

    return pl.pallas_call(
        kernel,
        out_shape=jax.ShapeDtypeStruct((8, 256), F32),
        in_specs=[ANYWHERE] * len(columns),
        out_specs=VMEM,
        scratch_shapes=[
            pltpu.VMEM((8 * ROWS, 256), jnp.bfloat16),
            pltpu.VMEM((8 * ROWS, ROWS), jnp.bfloat16),
            pltpu.SemaphoreType.DMA((2 * len(columns),)),
        ],
        compiler_params=SMALL,
        cost_estimate=pl.CostEstimate(flops=2**26, bytes_accessed=2**20, transcendentals=0),
    )(*columns.values())


def peak(value):
    top = jnp.maximum(jnp.max(jnp.abs(value)), 1e-30)
    return jnp.broadcast_to(top, (16, 256)).astype(jnp.bfloat16)


def encode(value, top):
    size = jnp.log2(jnp.maximum(jnp.abs(value) * (1.0 / top.astype(F32)[:1]), 2.0**-26))
    power = jnp.exp2(jnp.maximum(126.0 + 22.0 * size, 5.0 * size - 10.0))
    return jnp.where(value < 0, -power, power).astype(jnp.bfloat16)


def decode(code, top):
    code = code.astype(F32)
    size = jnp.log2(jnp.maximum(jnp.abs(code), 2.0**-126))
    value = jnp.exp2(jnp.minimum((size - 126.0) * (1.0 / 22.0), (size + 10.0) * 0.2)) * top.astype(F32)[:1]
    return jnp.where(code < 0, -value, jnp.where(code > 0, value, 0.0))


def split_yhi(keep, received, backs, cost):
    m = keep.shape[0]
    order = [backs.index(-back if -back in backs else back) for back in backs]

    def kernel(a, *refs):
        own, code = refs[len(received) :]
        b = jnp.concatenate([ref[...] for ref in refs[: len(received)]], axis=0)
        b = jnp.concatenate([b[ROWS * i : ROWS * (i + 1)] for i in order], axis=0)
        own[...] = a[:, :256] + b[:, :256]
        other = a[:, 256:] + b[:, 256:]
        top = peak(other)
        code[:m] = encode(other, top)
        code[m:] = top

    return pl.pallas_call(
        kernel,
        out_shape=(
            jax.ShapeDtypeStruct((m, 256), F32),
            jax.ShapeDtypeStruct((m + 16, 256), jnp.bfloat16),
        ),
        in_specs=[VMEM] * (1 + len(received)),
        out_specs=(VMEM, VMEM),
        compiler_params=SMALL,
        cost_estimate=takes(cost),
    )(keep, *received)


def split_z(own, received, last_rows, backs, cost):
    m = own.shape[0]

    def kernel(own, code, rows, *outs):
        full = own[...] + decode(code[:m], code[m:])
        left, parts = rows[:1], []
        for _ in range(3):
            parts.append(left.astype(jnp.bfloat16).astype(F32))
            left = left - parts[-1]
        row = lax.broadcasted_iota(jnp.int32, (16, 256), 0)
        for i, (back, out) in enumerate(zip(backs, outs)):
            block = full[ROWS * i : ROWS * (i + 1)]
            if back == 0:
                out[...] = block
                continue
            top = peak(block)
            out[:ROWS] = encode(block, top)
            tail = jnp.where(row == 0, top.astype(F32), 0.0)
            for j in range(3):
                tail = jnp.where(row == j + 1, parts[j], tail)
            out[ROWS:] = tail.astype(jnp.bfloat16)

    whole = jax.ShapeDtypeStruct((ROWS, 256), F32)
    coded = jax.ShapeDtypeStruct((ROWS + 16, 256), jnp.bfloat16)
    return pl.pallas_call(
        kernel,
        out_shape=tuple(coded if back else whole for back in backs),
        in_specs=[VMEM] * 3,
        out_specs=tuple(VMEM for _ in backs),
        compiler_params=SMALL,
        cost_estimate=takes(cost),
    )(own, received, last_rows)


def place(blocks, backs, last_rows):
    def kernel(*refs):
        rows, out, update = refs[len(blocks) :]
        total = rows[:1]
        for block, back in zip(refs, backs):
            z = lax.rem(lax.axis_index("z") + NZ + turn(back), NZ)
            at = pl.multiple_of(z * ROWS, ROWS)
            if back:
                tail = block[ROWS:]
                value = decode(block[:ROWS], tail)
                total = total + jnp.sum(tail[1:4].astype(F32), axis=0, keepdims=True)
            else:
                value = block[...]
            out[:, pl.ds(at, ROWS)] = value[:, :ROWS]
            out[:, pl.ds(at + NZ * ROWS, ROWS)] = value[:, ROWS:]
        owned = jnp.zeros((1, 32), F32)
        for z in range(NZ):
            owned = jnp.where(lax.axis_index("z") == z, total[:, 32 * z : 32 * z + 32], owned)
        update[...] = owned

    return pl.pallas_call(
        kernel,
        out_shape=(
            jax.ShapeDtypeStruct((ROWS, PANEL), F32),
            jax.ShapeDtypeStruct((1, 32), F32),
        ),
        in_specs=[VMEM] * (len(blocks) + 1),
        out_specs=(VMEM, VMEM),
        compiler_params=SMALL,
        cost_estimate=pl.CostEstimate(flops=0, bytes_accessed=2**21, transcendentals=0),
    )(*blocks, last_rows)


def body(log_derivs, sample_vector):
    scale_gram = 1.0 / math.sqrt(PANEL * 4)
    scale_update = 1.0 / math.sqrt(ROWS * 64)

    rows, columns = gather(log_derivs, pack(log_derivs, sample_vector))
    last_rows = term(scale_update, columns)

    blocks = {}
    for backs, parts, costs in zip(GROUPS, PARTS, COSTS):
        keep, *sends = products(scale_gram, [rows[back] for back in backs], columns, parts, costs[0])
        own, code = split_yhi(keep, [swap(send, "core") for send in sends], backs, costs[1])
        done = split_z(own, swap(code, "yhi"), last_rows, backs, costs[2])
        for back, block in zip(backs, done):
            blocks[back] = shift(block, "z", -back) if back else block
    return place(blocks.values(), list(blocks), last_rows)


def solution(mesh):
    fine = Mesh(mesh.devices.reshape(SIZES), AXES)
    samp, par = AXES[:3], AXES[3:]
    return jax.shard_map(
        body,
        mesh=fine,
        in_specs=(P(samp, par), P(samp)),
        out_specs=(P(samp, par), P(par, samp)),
        check_vma=False,
    )
```

```python
import math

import jax
import jax.numpy as jnp
from jax import lax
from jax.experimental import pallas as pl
from jax.experimental.pallas import tpu as pltpu
from jax.sharding import Mesh, PartitionSpec as P

AXES = ("ylo", "x", "z", "yhi", "core")
SIZES = (2, 4, 8, 2, 2)
ROWS, PANEL = 128, 2048
NX, NZ = 4, 8
F32 = jnp.float32
GROUPS = ((0, 1, -1, 2, -2), (3, -3, 4))
PARTS = ((160,) * 4, (128,) * 3)
COSTS = ((0, 0, 10), (1.1, 0.5, 0.5))
PLACE_COSTS = (0, 0)
VMEM = pl.BlockSpec(memory_space=pltpu.VMEM)
ANYWHERE = pl.BlockSpec(memory_space=pl.ANY)
SMALL = pltpu.CompilerParams(vmem_limit_bytes=16 * 2**20)


def takes(work):
    return pl.CostEstimate(flops=int(1e9 * work), bytes_accessed=0, transcendentals=0)


def shift(value, axis, by):
    size = SIZES[AXES.index(axis)]
    pairs = [(2 * i + c, 2 * ((i + (by, -by)[c]) % size) + c) for i in range(size) for c in range(2)]
    return lax.ppermute(value, (axis, "core"), pairs)


def swap(value, axis):
    return lax.ppermute(value, axis, [(0, 1), (1, 0)])


def turn(by):
    return by * (1 - 2 * lax.axis_index("core"))


def after(value, *others):
    return lax.optimization_barrier((value, *others))[0]


def gather(log_derivs, packed):
    z_a1, z_b1 = shift(log_derivs, "z", 1), shift(log_derivs, "z", -1)
    x_a0, x_b0 = shift(packed, "x", 1), shift(packed, "x", -1)
    partner = swap(packed, "ylo")

    z_a2, z_b2 = shift(z_a1, "z", 1), shift(z_b1, "z", -1)
    x_a1, x_far0 = shift(partner, "x", 1), shift(x_a0, "x", 1)
    x_b1 = swap(x_b0, "ylo")

    z_a3, z_b3 = shift(z_a2, "z", 1), shift(z_b2, "z", -1)
    x_far1 = shift(after(x_a1, x_far0, x_b1), "x", 1)

    z_a4 = shift(after(z_a3, z_b3), "z", 1)
    rows = {0: log_derivs, 1: z_a1, -1: z_b1, 2: z_a2, -2: z_b2, 3: z_a3, -3: z_b3, 4: z_a4}
    columns = {(0, 0): packed, (0, 1): x_a0, (0, -1): x_b0, (0, 2): x_far0}
    columns |= {(1, 0): partner, (1, 1): x_a1, (1, -1): x_b1, (1, 2): x_far1}
    return rows, columns


def pack(log_derivs, sample_vector):
    def kernel(entries, vec, out):
        out[:, :PANEL] = entries[...]
        left = jnp.transpose(jnp.broadcast_to(vec[...], (ROWS, ROWS)))
        lane = lax.broadcasted_iota(jnp.int32, (ROWS, ROWS), 1)
        parts = jnp.zeros((ROWS, ROWS), F32)
        for i in range(3):
            part = left.astype(jnp.bfloat16).astype(F32)
            left = left - part
            parts = jnp.where(lane == i, part, parts)
        out[:, PANEL:] = parts.astype(jnp.bfloat16)

    return pl.pallas_call(
        kernel,
        out_shape=jax.ShapeDtypeStruct((ROWS, PANEL + ROWS), jnp.bfloat16),
        in_specs=[VMEM] * 2,
        out_specs=VMEM,
        compiler_params=SMALL,
        cost_estimate=takes(0),
    )(log_derivs, sample_vector[None])


def products(scale, rows, columns, other, parts, cost):
    n = len(rows)

    def kernel(*refs):
        cols, outs, (held, sems) = refs[n : n + len(columns)], refs[n + len(columns) : -2], refs[-2:]
        copies = []
        for i, (ref, (ylo, back)) in enumerate(zip(cols, columns)):
            x = lax.rem(lax.axis_index("x") + NX - turn(back), NX)
            core = lax.rem(lax.div(x, 2) + lax.axis_index("core"), 2)
            yhi = lax.rem(lax.axis_index("ylo") + ylo + lax.axis_index("yhi"), 2)
            to = pl.multiple_of(lax.rem(x, 2) * ROWS, ROWS)
            copy = pltpu.make_async_copy(
                ref.at[:, pl.ds(0, PANEL)], held.at[yhi, pl.ds(to, ref.shape[0])], sems.at[i]
            )
            copies.append((core == other, copy))
        for mine, copy in copies:
            pl.when(mine)(copy.start)
        for mine, copy in copies:
            pl.when(mine)(copy.wait)
        block = jnp.concatenate([r[...] for r in refs[:n]], axis=0)
        for pair in range(2):
            value = scale * lax.dot_general(
                block, held[pair], (((1,), (1,)), ((), ())), preferred_element_type=F32
            )
            first = 0
            for out in outs:
                out[:, 256 * pair : 256 * pair + 256] = value[first : first + out.shape[0]]
                first += out.shape[0]

    return pl.pallas_call(
        kernel,
        out_shape=[jax.ShapeDtypeStruct((count, 512), F32) for count in parts],
        in_specs=[VMEM] * n + [ANYWHERE] * len(columns),
        out_specs=[VMEM] * len(parts),
        scratch_shapes=[
            pltpu.VMEM((2, 256, PANEL), jnp.bfloat16),
            pltpu.SemaphoreType.DMA((len(columns),)),
        ],
        compiler_params=pltpu.CompilerParams(vmem_limit_bytes=24 * 2**20),
        cost_estimate=takes(cost),
    )(*rows, *columns.values())


def term(scale, columns):
    def kernel(*refs):
        cols = refs[: len(columns)]
        out, held, vecs, sems = refs[len(columns) :]
        u = lax.axis_index("ylo") * NX + lax.axis_index("x")
        mine = pl.multiple_of(u * 256, 256)
        copies, to = [], 0
        for i, ref in enumerate(cols):
            for j, (part, target) in enumerate(((pl.ds(mine, 256), held), (pl.ds(PANEL, ROWS), vecs))):
                copy = pltpu.make_async_copy(
                    ref.at[:, part], target.at[pl.ds(to, ref.shape[0])], sems.at[2 * i + j]
                )
                copy.start()
                copies.append(copy)
            to += ref.shape[0]
        for copy in copies:
            copy.wait()
        parts = lax.dot_general(
            vecs[...], held[...], (((0,), (0,)), ((), ())), preferred_element_type=F32
        )
        out[...] = jnp.broadcast_to(scale * jnp.sum(parts, axis=0, keepdims=True), (8, 256))

    return pl.pallas_call(
        kernel,
        out_shape=jax.ShapeDtypeStruct((8, 256), F32),
        in_specs=[ANYWHERE] * len(columns),
        out_specs=VMEM,
        scratch_shapes=[
            pltpu.VMEM((8 * ROWS, 256), jnp.bfloat16),
            pltpu.VMEM((8 * ROWS, ROWS), jnp.bfloat16),
            pltpu.SemaphoreType.DMA((2 * len(columns),)),
        ],
        compiler_params=SMALL,
        cost_estimate=pl.CostEstimate(flops=2**26, bytes_accessed=2**20, transcendentals=0),
    )(*columns.values())


def peak(value):
    top = jnp.maximum(jnp.max(jnp.abs(value)), 1e-30)
    return jnp.broadcast_to(top, (16, 256)).astype(jnp.bfloat16)


def encode(value, top):
    size = jnp.log2(jnp.maximum(jnp.abs(value) * (1.0 / top.astype(F32)[:1]), 2.0**-26))
    power = jnp.exp2(jnp.maximum(126.0 + 22.0 * size, 5.0 * size - 10.0))
    return jnp.where(value < 0, -power, power).astype(jnp.bfloat16)


def decode(code, top):
    code = code.astype(F32)
    size = jnp.log2(jnp.maximum(jnp.abs(code), 2.0**-126))
    value = jnp.exp2(jnp.minimum((size - 126.0) * (1.0 / 22.0), (size + 10.0) * 0.2)) * top.astype(F32)[:1]
    return jnp.where(code < 0, -value, jnp.where(code > 0, value, 0.0))


def split_yhi(keep, received, backs, cost):
    m = keep.shape[0]
    order = [backs.index(-back if -back in backs else back) for back in backs]

    def kernel(a, *refs):
        own, code = refs[len(received) :]
        b = jnp.concatenate([ref[...] for ref in refs[: len(received)]], axis=0)
        b = jnp.concatenate([b[ROWS * i : ROWS * (i + 1)] for i in order], axis=0)
        own[...] = a[:, :256] + b[:, :256]
        other = a[:, 256:] + b[:, 256:]
        top = peak(other)
        code[:m] = encode(other, top)
        code[m:] = top

    return pl.pallas_call(
        kernel,
        out_shape=(
            jax.ShapeDtypeStruct((m, 256), F32),
            jax.ShapeDtypeStruct((m + 16, 256), jnp.bfloat16),
        ),
        in_specs=[VMEM] * (1 + len(received)),
        out_specs=(VMEM, VMEM),
        compiler_params=SMALL,
        cost_estimate=takes(cost),
    )(keep, *received)


def split_z(own, received, last_rows, backs, cost):
    m = own.shape[0]

    def kernel(own, code, rows, *outs):
        full = own[...] + decode(code[:m], code[m:])
        left, parts = rows[:1], []
        for _ in range(3):
            parts.append(left.astype(jnp.bfloat16).astype(F32))
            left = left - parts[-1]
        row = lax.broadcasted_iota(jnp.int32, (16, 256), 0)
        for i, (back, out) in enumerate(zip(backs, outs)):
            block = full[ROWS * i : ROWS * (i + 1)]
            if back == 0:
                out[...] = block
                continue
            top = peak(block)
            out[:ROWS] = encode(block, top)
            tail = jnp.where(row == 0, top.astype(F32), 0.0)
            for j in range(3):
                tail = jnp.where(row == j + 1, parts[j], tail)
            out[ROWS:] = tail.astype(jnp.bfloat16)

    whole = jax.ShapeDtypeStruct((ROWS, 256), F32)
    coded = jax.ShapeDtypeStruct((ROWS + 16, 256), jnp.bfloat16)
    return pl.pallas_call(
        kernel,
        out_shape=tuple(coded if back else whole for back in backs),
        in_specs=[VMEM] * 3,
        out_specs=tuple(VMEM for _ in backs),
        compiler_params=SMALL,
        cost_estimate=takes(cost),
    )(own, received, last_rows)


def place(blocks, total, gram, last, cost):
    n, held = len(blocks), [] if gram is None else [gram]

    def kernel(*refs):
        out, result, stage, sems = refs[n + 1 + len(held) :]
        sum_of = refs[n][:1]
        copies = []
        for i, (block, back) in enumerate(zip(refs, blocks)):
            z = lax.rem(lax.axis_index("z") + NZ + turn(back), NZ)
            at = pl.multiple_of(z * ROWS, ROWS)
            if back:
                tail = block[ROWS:]
                stage[i] = decode(block[:ROWS], tail)
                sum_of = sum_of + jnp.sum(tail[1:4].astype(F32), axis=0, keepdims=True)
            else:
                stage[i] = block[...]
            for odd in range(2):
                copy = pltpu.make_async_copy(
                    stage.at[i, :, pl.ds(odd * ROWS, ROWS)],
                    out.at[:, pl.ds(at + odd * NZ * ROWS, ROWS)],
                    sems.at[i, odd],
                )
                copy.start()
                copies.append(copy)
        if last:
            turned = pltpu.roll(jnp.broadcast_to(sum_of, (8, 256)), 256 - 32 * lax.axis_index("z"), 1)
            result[...] = turned[:1, :32]
        else:
            result[...] = jnp.broadcast_to(sum_of, (8, 256))
        for copy in copies:
            copy.wait()

    return pl.pallas_call(
        kernel,
        out_shape=(
            jax.ShapeDtypeStruct((ROWS, PANEL), F32),
            jax.ShapeDtypeStruct((1, 32) if last else (8, 256), F32),
        ),
        in_specs=[VMEM] * (n + 1) + [ANYWHERE] * len(held),
        out_specs=(ANYWHERE, VMEM),
        scratch_shapes=[pltpu.VMEM((n, ROWS, 256), F32), pltpu.SemaphoreType.DMA((n, 2))],
        input_output_aliases={n + 1: 0} if held else {},
        compiler_params=SMALL,
        cost_estimate=takes(cost),
    )(*blocks.values(), total, *held)


def body(log_derivs, sample_vector):
    scale_gram = 1.0 / math.sqrt(PANEL * 4)
    scale_update = 1.0 / math.sqrt(ROWS * 64)

    rows, columns = gather(log_derivs, pack(log_derivs, sample_vector))
    last_rows = term(scale_update, columns)

    blocks = {}
    for backs, parts, costs in zip(GROUPS, PARTS, COSTS):
        factors = [rows[back] for back in backs]
        sends = products(scale_gram, factors, columns, 1, parts, costs[0])
        received = [swap(send, "core") for send in sends]
        (keep,) = products(scale_gram, factors, columns, 0, (sum(parts),), costs[0])
        own, code = split_yhi(keep, received, backs, costs[1])
        done = split_z(own, swap(code, "yhi"), last_rows, backs, costs[2])
        for back, block in zip(backs, done):
            blocks[back] = shift(block, "z", -back) if back else block

    gram, total = None, last_rows
    for backs, cost in zip(GROUPS, PLACE_COSTS):
        gram, total = place({back: blocks[back] for back in backs}, total, gram, backs == GROUPS[-1], cost)
    return gram, total


def solution(mesh):
    fine = Mesh(mesh.devices.reshape(SIZES), AXES)
    samp, par = AXES[:3], AXES[3:]
    return jax.shard_map(
        body,
        mesh=fine,
        in_specs=(P(samp, par), P(samp)),
        out_specs=(P(samp, par), P(par, samp)),
        check_vma=False,
    )
```

```python
import math

import jax
import jax.numpy as jnp
from jax import lax
from jax.experimental import pallas as pl
from jax.experimental.pallas import tpu as pltpu
from jax.sharding import Mesh, PartitionSpec as P

AXES = ("ylo", "x", "z", "yhi", "core")
SIZES = (2, 4, 8, 2, 2)
ROWS, PANEL = 128, 2048
NX, NZ = 4, 8
F32 = jnp.float32
GROUPS = ((0, 1, -1, 2, -2), (3, -3, 4))
PARTS = ((160,) * 4, (128,) * 3)
COSTS = ((0, 0, 10), (1.1, 0.5, 0.5))
PLACE_COSTS = (0, 0)
VMEM = pl.BlockSpec(memory_space=pltpu.VMEM)
ANYWHERE = pl.BlockSpec(memory_space=pl.ANY)
SMALL = pltpu.CompilerParams(vmem_limit_bytes=16 * 2**20)


def takes(work):
    return pl.CostEstimate(flops=int(1e9 * work), bytes_accessed=0, transcendentals=0)


def shift(value, axis, by):
    size = SIZES[AXES.index(axis)]
    pairs = [(2 * i + c, 2 * ((i + (by, -by)[c]) % size) + c) for i in range(size) for c in range(2)]
    return lax.ppermute(value, (axis, "core"), pairs)


def swap(value, axis):
    return lax.ppermute(value, axis, [(0, 1), (1, 0)])


def turn(by):
    return by * (1 - 2 * lax.axis_index("core"))


def after(value, *others):
    return lax.optimization_barrier((value, *others))[0]


def gather(log_derivs, packed):
    z_a1, z_b1 = shift(log_derivs, "z", 1), shift(log_derivs, "z", -1)
    x_a0, x_b0 = shift(packed, "x", 1), shift(packed, "x", -1)
    partner = swap(packed, "ylo")

    z_a2, z_b2 = shift(z_a1, "z", 1), shift(z_b1, "z", -1)
    x_a1, x_far0 = shift(partner, "x", 1), shift(x_a0, "x", 1)
    x_b1 = swap(x_b0, "ylo")

    z_a3, z_b3 = shift(z_a2, "z", 1), shift(z_b2, "z", -1)
    x_far1 = shift(after(x_a1, x_far0, x_b1), "x", 1)

    z_a4 = shift(after(z_a3, z_b3), "z", 1)
    rows = {0: log_derivs, 1: z_a1, -1: z_b1, 2: z_a2, -2: z_b2, 3: z_a3, -3: z_b3, 4: z_a4}
    columns = {(0, 0): packed, (0, 1): x_a0, (0, -1): x_b0, (0, 2): x_far0}
    columns |= {(1, 0): partner, (1, 1): x_a1, (1, -1): x_b1, (1, 2): x_far1}
    return rows, columns


def pack(log_derivs, sample_vector):
    def kernel(entries, vec, out):
        out[:, :PANEL] = entries[...]
        left = jnp.transpose(jnp.broadcast_to(vec[...], (ROWS, ROWS)))
        lane = lax.broadcasted_iota(jnp.int32, (ROWS, ROWS), 1)
        parts = jnp.zeros((ROWS, ROWS), F32)
        for i in range(3):
            part = left.astype(jnp.bfloat16).astype(F32)
            left = left - part
            parts = jnp.where(lane == i, part, parts)
        out[:, PANEL:] = parts.astype(jnp.bfloat16)

    return pl.pallas_call(
        kernel,
        out_shape=jax.ShapeDtypeStruct((ROWS, PANEL + ROWS), jnp.bfloat16),
        in_specs=[VMEM] * 2,
        out_specs=VMEM,
        compiler_params=SMALL,
        cost_estimate=takes(0),
    )(log_derivs, sample_vector[None])


def products(scale, rows, columns, other, parts, cost):
    n = len(rows)

    def kernel(*refs):
        cols, outs, (held, sems) = refs[n : n + len(columns)], refs[n + len(columns) : -2], refs[-2:]
        copies = []
        for i, (ref, (ylo, back)) in enumerate(zip(cols, columns)):
            x = lax.rem(lax.axis_index("x") + NX - turn(back), NX)
            core = lax.rem(lax.div(x, 2) + lax.axis_index("core"), 2)
            yhi = lax.rem(lax.axis_index("ylo") + ylo + lax.axis_index("yhi"), 2)
            to = pl.multiple_of(lax.rem(x, 2) * ROWS, ROWS)
            copy = pltpu.make_async_copy(
                ref.at[:, pl.ds(0, PANEL)], held.at[yhi, pl.ds(to, ref.shape[0])], sems.at[i]
            )
            copies.append((core == other, copy))
        for mine, copy in copies:
            pl.when(mine)(copy.start)
        for mine, copy in copies:
            pl.when(mine)(copy.wait)
        block = jnp.concatenate([r[...] for r in refs[:n]], axis=0)
        for pair in range(2):
            value = scale * lax.dot_general(
                block, held[pair], (((1,), (1,)), ((), ())), preferred_element_type=F32
            )
            first = 0
            for out in outs:
                out[:, 256 * pair : 256 * pair + 256] = value[first : first + out.shape[0]]
                first += out.shape[0]

    return pl.pallas_call(
        kernel,
        out_shape=[jax.ShapeDtypeStruct((count, 512), F32) for count in parts],
        in_specs=[VMEM] * n + [ANYWHERE] * len(columns),
        out_specs=[VMEM] * len(parts),
        scratch_shapes=[
            pltpu.VMEM((2, 256, PANEL), jnp.bfloat16),
            pltpu.SemaphoreType.DMA((len(columns),)),
        ],
        compiler_params=pltpu.CompilerParams(vmem_limit_bytes=24 * 2**20),
        cost_estimate=takes(cost),
    )(*rows, *columns.values())


def term(scale, columns):
    def kernel(*refs):
        cols = refs[: len(columns)]
        out, held, vecs, sems = refs[len(columns) :]
        u = lax.axis_index("ylo") * NX + lax.axis_index("x")
        mine = pl.multiple_of(u * 256, 256)
        copies, to = [], 0
        for i, ref in enumerate(cols):
            for j, (part, target) in enumerate(((pl.ds(mine, 256), held), (pl.ds(PANEL, ROWS), vecs))):
                copy = pltpu.make_async_copy(
                    ref.at[:, part], target.at[pl.ds(to, ref.shape[0])], sems.at[2 * i + j]
                )
                copy.start()
                copies.append(copy)
            to += ref.shape[0]
        for copy in copies:
            copy.wait()
        parts = lax.dot_general(
            vecs[...], held[...], (((0,), (0,)), ((), ())), preferred_element_type=F32
        )
        out[...] = jnp.broadcast_to(scale * jnp.sum(parts, axis=0, keepdims=True), (8, 256))

    return pl.pallas_call(
        kernel,
        out_shape=jax.ShapeDtypeStruct((8, 256), F32),
        in_specs=[ANYWHERE] * len(columns),
        out_specs=VMEM,
        scratch_shapes=[
            pltpu.VMEM((8 * ROWS, 256), jnp.bfloat16),
            pltpu.VMEM((8 * ROWS, ROWS), jnp.bfloat16),
            pltpu.SemaphoreType.DMA((2 * len(columns),)),
        ],
        compiler_params=SMALL,
        cost_estimate=pl.CostEstimate(flops=2**26, bytes_accessed=2**20, transcendentals=0),
    )(*columns.values())


def peak(value):
    top = jnp.maximum(jnp.max(jnp.abs(value)), 1e-30)
    return jnp.broadcast_to(top, (16, 256)).astype(jnp.bfloat16)


def encode(value, top):
    size = jnp.log2(jnp.maximum(jnp.abs(value) * (1.0 / top.astype(F32)[:1]), 2.0**-26))
    power = jnp.exp2(jnp.maximum(126.0 + 22.0 * size, 5.0 * size - 10.0))
    return jnp.where(value < 0, -power, power).astype(jnp.bfloat16)


def decode(code, top):
    code = code.astype(F32)
    size = jnp.log2(jnp.maximum(jnp.abs(code), 2.0**-126))
    value = jnp.exp2(jnp.minimum((size - 126.0) * (1.0 / 22.0), (size + 10.0) * 0.2)) * top.astype(F32)[:1]
    return jnp.where(code < 0, -value, jnp.where(code > 0, value, 0.0))


def split_yhi(keep, received, backs, cost):
    m = keep.shape[0]
    order = [backs.index(-back if -back in backs else back) for back in backs]

    def kernel(a, *refs):
        own, code = refs[len(received) :]
        b = jnp.concatenate([ref[...] for ref in refs[: len(received)]], axis=0)
        b = jnp.concatenate([b[ROWS * i : ROWS * (i + 1)] for i in order], axis=0)
        own[...] = a[:, :256] + b[:, :256]
        other = a[:, 256:] + b[:, 256:]
        top = peak(other)
        code[:m] = encode(other, top)
        code[m:] = top

    return pl.pallas_call(
        kernel,
        out_shape=(
            jax.ShapeDtypeStruct((m, 256), F32),
            jax.ShapeDtypeStruct((m + 16, 256), jnp.bfloat16),
        ),
        in_specs=[VMEM] * (1 + len(received)),
        out_specs=(VMEM, VMEM),
        compiler_params=SMALL,
        cost_estimate=takes(cost),
    )(keep, *received)


def split_z(own, received, last_rows, backs, cost):
    m = own.shape[0]

    def kernel(own, code, rows, *outs):
        full = own[...] + decode(code[:m], code[m:])
        left, parts = rows[:1], []
        for _ in range(3):
            parts.append(left.astype(jnp.bfloat16).astype(F32))
            left = left - parts[-1]
        row = lax.broadcasted_iota(jnp.int32, (16, 256), 0)
        for i, (back, out) in enumerate(zip(backs, outs)):
            block = full[ROWS * i : ROWS * (i + 1)]
            if back == 0:
                out[...] = block
                continue
            top = peak(block)
            out[:ROWS] = encode(block, top)
            tail = jnp.where(row == 0, top.astype(F32), 0.0)
            for j in range(3):
                tail = jnp.where(row == j + 1, parts[j], tail)
            out[ROWS:] = tail.astype(jnp.bfloat16)

    whole = jax.ShapeDtypeStruct((ROWS, 256), F32)
    coded = jax.ShapeDtypeStruct((ROWS + 16, 256), jnp.bfloat16)
    return pl.pallas_call(
        kernel,
        out_shape=tuple(coded if back else whole for back in backs),
        in_specs=[VMEM] * 3,
        out_specs=tuple(VMEM for _ in backs),
        compiler_params=SMALL,
        cost_estimate=takes(cost),
    )(own, received, last_rows)


def place(blocks, total, gram, last, cost):
    n, held = len(blocks), [] if gram is None else [gram]

    def kernel(*refs):
        out, result, stage, sems = refs[n + 1 + len(held) :]
        sum_of = refs[n][:1]
        copies = []
        for i, (block, back) in enumerate(zip(refs, blocks)):
            z = lax.rem(lax.axis_index("z") + NZ + turn(back), NZ)
            at = pl.multiple_of(z * ROWS, ROWS)
            if back:
                tail = block[ROWS:]
                stage[i] = decode(block[:ROWS], tail)
                sum_of = sum_of + jnp.sum(tail[1:4].astype(F32), axis=0, keepdims=True)
            else:
                stage[i] = block[...]
            for odd in range(2):
                copy = pltpu.make_async_copy(
                    stage.at[i, :, pl.ds(odd * ROWS, ROWS)],
                    out.at[:, pl.ds(at + odd * NZ * ROWS, ROWS)],
                    sems.at[i, odd],
                )
                copy.start()
                copies.append(copy)
        if last:
            turned = pltpu.roll(jnp.broadcast_to(sum_of, (8, 256)), lax.rem(256 - 32 * lax.axis_index("z"), 256), 1)
            result[...] = turned[:1, :32]
        else:
            result[...] = jnp.broadcast_to(sum_of, (8, 256))
        for copy in copies:
            copy.wait()

    return pl.pallas_call(
        kernel,
        out_shape=(
            jax.ShapeDtypeStruct((ROWS, PANEL), F32),
            jax.ShapeDtypeStruct((1, 32) if last else (8, 256), F32),
        ),
        in_specs=[VMEM] * (n + 1) + [ANYWHERE] * len(held),
        out_specs=(ANYWHERE, VMEM),
        scratch_shapes=[pltpu.VMEM((n, ROWS, 256), F32), pltpu.SemaphoreType.DMA((n, 2))],
        input_output_aliases={n + 1: 0} if held else {},
        compiler_params=SMALL,
        cost_estimate=takes(cost),
    )(*blocks.values(), total, *held)


def body(log_derivs, sample_vector):
    scale_gram = 1.0 / math.sqrt(PANEL * 4)
    scale_update = 1.0 / math.sqrt(ROWS * 64)

    rows, columns = gather(log_derivs, pack(log_derivs, sample_vector))
    last_rows = term(scale_update, columns)

    blocks = {}
    for backs, parts, costs in zip(GROUPS, PARTS, COSTS):
        factors = [rows[back] for back in backs]
        sends = products(scale_gram, factors, columns, 1, parts, costs[0])
        received = [swap(send, "core") for send in sends]
        (keep,) = products(scale_gram, factors, columns, 0, (sum(parts),), costs[0])
        own, code = split_yhi(keep, received, backs, costs[1])
        done = split_z(own, swap(code, "yhi"), last_rows, backs, costs[2])
        for back, block in zip(backs, done):
            blocks[back] = shift(block, "z", -back) if back else block

    gram, total = None, last_rows
    for backs, cost in zip(GROUPS, PLACE_COSTS):
        gram, total = place({back: blocks[back] for back in backs}, total, gram, backs == GROUPS[-1], cost)
    return gram, total


def solution(mesh):
    fine = Mesh(mesh.devices.reshape(SIZES), AXES)
    samp, par = AXES[:3], AXES[3:]
    return jax.shard_map(
        body,
        mesh=fine,
        in_specs=(P(samp, par), P(samp)),
        out_specs=(P(samp, par), P(par, samp)),
        check_vma=False,
    )
```

```python
import math

import jax
import jax.numpy as jnp
from jax import lax
from jax.experimental import pallas as pl
from jax.experimental.pallas import tpu as pltpu
from jax.sharding import Mesh, PartitionSpec as P

AXES = ("ylo", "x", "z", "yhi", "core")
SIZES = (2, 4, 8, 2, 2)
ROWS, PANEL = 128, 2048
NX, NZ = 4, 8
F32 = jnp.float32
GROUPS = ((0, 1, -1, 2, -2), (3, -3, 4))
PARTS = ((160,) * 4, (128,) * 3)
COSTS = ((0, 0, 10), (1.1, 0.5, 0.5))
PLACE_COSTS = (0, 0)
VMEM = pl.BlockSpec(memory_space=pltpu.VMEM)
ANYWHERE = pl.BlockSpec(memory_space=pl.ANY)
SMALL = pltpu.CompilerParams(vmem_limit_bytes=16 * 2**20)


def takes(work):
    return pl.CostEstimate(flops=int(1e9 * work), bytes_accessed=0, transcendentals=0)


def shift(value, axis, by):
    size = SIZES[AXES.index(axis)]
    pairs = [(2 * i + c, 2 * ((i + (by, -by)[c]) % size) + c) for i in range(size) for c in range(2)]
    return lax.ppermute(value, (axis, "core"), pairs)


def swap(value, axis):
    return lax.ppermute(value, axis, [(0, 1), (1, 0)])


def turn(by):
    return by * (1 - 2 * lax.axis_index("core"))


def after(value, *others):
    return lax.optimization_barrier((value, *others))[0]


def gather(log_derivs, packed):
    z_a1, z_b1 = shift(log_derivs, "z", 1), shift(log_derivs, "z", -1)
    x_a0, x_b0 = shift(packed, "x", 1), shift(packed, "x", -1)
    partner = swap(packed, "ylo")

    z_a2, z_b2 = shift(z_a1, "z", 1), shift(z_b1, "z", -1)
    x_a1, x_far0 = shift(partner, "x", 1), shift(x_a0, "x", 1)
    x_b1 = swap(x_b0, "ylo")

    z_a3, z_b3 = shift(z_a2, "z", 1), shift(z_b2, "z", -1)
    x_far1 = shift(after(x_a1, x_far0, x_b1), "x", 1)

    z_a4 = shift(after(z_a3, z_b3), "z", 1)
    rows = {0: log_derivs, 1: z_a1, -1: z_b1, 2: z_a2, -2: z_b2, 3: z_a3, -3: z_b3, 4: z_a4}
    columns = {(0, 0): packed, (0, 1): x_a0, (0, -1): x_b0, (0, 2): x_far0}
    columns |= {(1, 0): partner, (1, 1): x_a1, (1, -1): x_b1, (1, 2): x_far1}
    return rows, columns


def pack(log_derivs, sample_vector):
    def kernel(vec, out):
        left = jnp.transpose(jnp.broadcast_to(vec[...], (ROWS, ROWS)))
        lane = lax.broadcasted_iota(jnp.int32, (ROWS, ROWS), 1)
        parts = jnp.zeros((ROWS, ROWS), F32)
        for i in range(3):
            part = left.astype(jnp.bfloat16).astype(F32)
            left = left - part
            parts = jnp.where(lane == i, part, parts)
        out[...] = parts.astype(jnp.bfloat16)

    parts = pl.pallas_call(
        kernel,
        out_shape=jax.ShapeDtypeStruct((ROWS, ROWS), jnp.bfloat16),
        in_specs=[VMEM],
        out_specs=VMEM,
        compiler_params=SMALL,
        cost_estimate=takes(0),
    )(sample_vector[None])
    return jnp.concatenate([log_derivs, parts], axis=1)


def products(scale, rows, columns, other, parts, cost):
    n = len(rows)

    def kernel(*refs):
        cols, outs, (held, sems) = refs[n : n + len(columns)], refs[n + len(columns) : -2], refs[-2:]
        copies = []
        for i, (ref, (ylo, back)) in enumerate(zip(cols, columns)):
            x = lax.rem(lax.axis_index("x") + NX - turn(back), NX)
            core = lax.rem(lax.div(x, 2) + lax.axis_index("core"), 2)
            yhi = lax.rem(lax.axis_index("ylo") + ylo + lax.axis_index("yhi"), 2)
            to = pl.multiple_of(lax.rem(x, 2) * ROWS, ROWS)
            copy = pltpu.make_async_copy(
                ref.at[:, pl.ds(0, PANEL)], held.at[yhi, pl.ds(to, ref.shape[0])], sems.at[i]
            )
            copies.append((core == other, copy))
        for mine, copy in copies:
            pl.when(mine)(copy.start)
        for mine, copy in copies:
            pl.when(mine)(copy.wait)
        block = jnp.concatenate([r[...] for r in refs[:n]], axis=0)
        for pair in range(2):
            value = scale * lax.dot_general(
                block, held[pair], (((1,), (1,)), ((), ())), preferred_element_type=F32
            )
            first = 0
            for out in outs:
                out[:, 256 * pair : 256 * pair + 256] = value[first : first + out.shape[0]]
                first += out.shape[0]

    return pl.pallas_call(
        kernel,
        out_shape=[jax.ShapeDtypeStruct((count, 512), F32) for count in parts],
        in_specs=[VMEM] * n + [ANYWHERE] * len(columns),
        out_specs=[VMEM] * len(parts),
        scratch_shapes=[
            pltpu.VMEM((2, 256, PANEL), jnp.bfloat16),
            pltpu.SemaphoreType.DMA((len(columns),)),
        ],
        compiler_params=pltpu.CompilerParams(vmem_limit_bytes=24 * 2**20),
        cost_estimate=takes(cost),
    )(*rows, *columns.values())


def term(scale, columns):
    def kernel(*refs):
        cols = refs[: len(columns)]
        out, held, vecs, sems = refs[len(columns) :]
        u = lax.axis_index("ylo") * NX + lax.axis_index("x")
        mine = pl.multiple_of(u * 256, 256)
        copies, to = [], 0
        for i, ref in enumerate(cols):
            for j, (part, target) in enumerate(((pl.ds(mine, 256), held), (pl.ds(PANEL, ROWS), vecs))):
                copy = pltpu.make_async_copy(
                    ref.at[:, part], target.at[pl.ds(to, ref.shape[0])], sems.at[2 * i + j]
                )
                copy.start()
                copies.append(copy)
            to += ref.shape[0]
        for copy in copies:
            copy.wait()
        parts = lax.dot_general(
            vecs[...], held[...], (((0,), (0,)), ((), ())), preferred_element_type=F32
        )
        out[...] = jnp.broadcast_to(scale * jnp.sum(parts, axis=0, keepdims=True), (8, 256))

    return pl.pallas_call(
        kernel,
        out_shape=jax.ShapeDtypeStruct((8, 256), F32),
        in_specs=[ANYWHERE] * len(columns),
        out_specs=VMEM,
        scratch_shapes=[
            pltpu.VMEM((8 * ROWS, 256), jnp.bfloat16),
            pltpu.VMEM((8 * ROWS, ROWS), jnp.bfloat16),
            pltpu.SemaphoreType.DMA((2 * len(columns),)),
        ],
        compiler_params=SMALL,
        cost_estimate=pl.CostEstimate(flops=2**26, bytes_accessed=2**20, transcendentals=0),
    )(*columns.values())


def peak(value):
    top = jnp.maximum(jnp.max(jnp.abs(value)), 1e-30)
    return jnp.broadcast_to(top, (16, 256)).astype(jnp.bfloat16)


def encode(value, top):
    size = jnp.log2(jnp.maximum(jnp.abs(value) * (1.0 / top.astype(F32)[:1]), 2.0**-26))
    power = jnp.exp2(jnp.maximum(126.0 + 22.0 * size, 5.0 * size - 10.0))
    return jnp.where(value < 0, -power, power).astype(jnp.bfloat16)


def decode(code, top):
    code = code.astype(F32)
    size = jnp.log2(jnp.maximum(jnp.abs(code), 2.0**-126))
    value = jnp.exp2(jnp.minimum((size - 126.0) * (1.0 / 22.0), (size + 10.0) * 0.2)) * top.astype(F32)[:1]
    return jnp.where(code < 0, -value, jnp.where(code > 0, value, 0.0))


def split_yhi(keep, received, backs, cost):
    m = keep.shape[0]
    order = [backs.index(-back if -back in backs else back) for back in backs]

    def kernel(a, *refs):
        own, code = refs[len(received) :]
        b = jnp.concatenate([ref[...] for ref in refs[: len(received)]], axis=0)
        b = jnp.concatenate([b[ROWS * i : ROWS * (i + 1)] for i in order], axis=0)
        own[...] = a[:, :256] + b[:, :256]
        other = a[:, 256:] + b[:, 256:]
        top = peak(other)
        code[:m] = encode(other, top)
        code[m:] = top

    return pl.pallas_call(
        kernel,
        out_shape=(
            jax.ShapeDtypeStruct((m, 256), F32),
            jax.ShapeDtypeStruct((m + 16, 256), jnp.bfloat16),
        ),
        in_specs=[VMEM] * (1 + len(received)),
        out_specs=(VMEM, VMEM),
        compiler_params=SMALL,
        cost_estimate=takes(cost),
    )(keep, *received)


def split_z(own, received, last_rows, backs, cost):
    m = own.shape[0]

    def kernel(own, code, rows, *outs):
        full = own[...] + decode(code[:m], code[m:])
        left, parts = rows[:1], []
        for _ in range(3):
            parts.append(left.astype(jnp.bfloat16).astype(F32))
            left = left - parts[-1]
        row = lax.broadcasted_iota(jnp.int32, (16, 256), 0)
        for i, (back, out) in enumerate(zip(backs, outs)):
            block = full[ROWS * i : ROWS * (i + 1)]
            if back == 0:
                out[...] = block
                continue
            top = peak(block)
            out[:ROWS] = encode(block, top)
            tail = jnp.where(row == 0, top.astype(F32), 0.0)
            for j in range(3):
                tail = jnp.where(row == j + 1, parts[j], tail)
            out[ROWS:] = tail.astype(jnp.bfloat16)

    whole = jax.ShapeDtypeStruct((ROWS, 256), F32)
    coded = jax.ShapeDtypeStruct((ROWS + 16, 256), jnp.bfloat16)
    return pl.pallas_call(
        kernel,
        out_shape=tuple(coded if back else whole for back in backs),
        in_specs=[VMEM] * 3,
        out_specs=tuple(VMEM for _ in backs),
        compiler_params=SMALL,
        cost_estimate=takes(cost),
    )(own, received, last_rows)


def place(blocks, total, gram, last, cost):
    n, held = len(blocks), [] if gram is None else [gram]

    def kernel(*refs):
        out, result, stage, sems = refs[n + 1 + len(held) :]
        sum_of = refs[n][:1]
        copies = []
        for i, (block, back) in enumerate(zip(refs, blocks)):
            z = lax.rem(lax.axis_index("z") + NZ + turn(back), NZ)
            at = pl.multiple_of(z * ROWS, ROWS)
            if back:
                tail = block[ROWS:]
                stage[i] = decode(block[:ROWS], tail)
                sum_of = sum_of + jnp.sum(tail[1:4].astype(F32), axis=0, keepdims=True)
            else:
                stage[i] = block[...]
            for odd in range(2):
                copy = pltpu.make_async_copy(
                    stage.at[i, :, pl.ds(odd * ROWS, ROWS)],
                    out.at[:, pl.ds(at + odd * NZ * ROWS, ROWS)],
                    sems.at[i, odd],
                )
                copy.start()
                copies.append(copy)
        if last:
            turned = pltpu.roll(jnp.broadcast_to(sum_of, (8, 256)), lax.rem(256 - 32 * lax.axis_index("z"), 256), 1)
            result[...] = turned[:1, :32]
        else:
            result[...] = jnp.broadcast_to(sum_of, (8, 256))
        for copy in copies:
            copy.wait()

    return pl.pallas_call(
        kernel,
        out_shape=(
            jax.ShapeDtypeStruct((ROWS, PANEL), F32),
            jax.ShapeDtypeStruct((1, 32) if last else (8, 256), F32),
        ),
        in_specs=[VMEM] * (n + 1) + [ANYWHERE] * len(held),
        out_specs=(ANYWHERE, VMEM),
        scratch_shapes=[pltpu.VMEM((n, ROWS, 256), F32), pltpu.SemaphoreType.DMA((n, 2))],
        input_output_aliases={n + 1: 0} if held else {},
        compiler_params=SMALL,
        cost_estimate=takes(cost),
    )(*blocks.values(), total, *held)


def body(log_derivs, sample_vector):
    scale_gram = 1.0 / math.sqrt(PANEL * 4)
    scale_update = 1.0 / math.sqrt(ROWS * 64)

    rows, columns = gather(log_derivs, pack(log_derivs, sample_vector))
    last_rows = term(scale_update, columns)

    blocks = {}
    for backs, parts, costs in zip(GROUPS, PARTS, COSTS):
        factors = [rows[back] for back in backs]
        sends = products(scale_gram, factors, columns, 1, parts, costs[0])
        received = [swap(send, "core") for send in sends]
        (keep,) = products(scale_gram, factors, columns, 0, (sum(parts),), costs[0])
        own, code = split_yhi(keep, received, backs, costs[1])
        done = split_z(own, swap(code, "yhi"), last_rows, backs, costs[2])
        for back, block in zip(backs, done):
            blocks[back] = shift(block, "z", -back) if back else block

    gram, total = None, last_rows
    for backs, cost in zip(GROUPS, PLACE_COSTS):
        gram, total = place({back: blocks[back] for back in backs}, total, gram, backs == GROUPS[-1], cost)
    return gram, total


def solution(mesh):
    fine = Mesh(mesh.devices.reshape(SIZES), AXES)
    samp, par = AXES[:3], AXES[3:]
    return jax.shard_map(
        body,
        mesh=fine,
        in_specs=(P(samp, par), P(samp)),
        out_specs=(P(samp, par), P(par, samp)),
        check_vma=False,
    )
```

```python
import math

import jax
import jax.numpy as jnp
from jax import lax
from jax.experimental import pallas as pl
from jax.experimental.pallas import tpu as pltpu
from jax.sharding import Mesh, PartitionSpec as P

AXES = ("ylo", "x", "z", "yhi", "core")
SIZES = (2, 4, 8, 2, 2)
ROWS, PANEL = 128, 2048
NX, NZ = 4, 8
F32 = jnp.float32
GROUPS = ((0, 2, -2, 1, -1), (3, -3, 4))
PARTS = ((160,) * 4, (128,) * 3)
COSTS = ((0, 0, 10), (1.1, 0.5, 0.5))
PLACE_COSTS = (0, 0)
VMEM = pl.BlockSpec(memory_space=pltpu.VMEM)
ANYWHERE = pl.BlockSpec(memory_space=pl.ANY)
SMALL = pltpu.CompilerParams(vmem_limit_bytes=16 * 2**20)


def takes(work):
    return pl.CostEstimate(flops=int(1e9 * work), bytes_accessed=0, transcendentals=0)


def shift(value, axis, by):
    size = SIZES[AXES.index(axis)]
    pairs = [(2 * i + c, 2 * ((i + (by, -by)[c]) % size) + c) for i in range(size) for c in range(2)]
    return lax.ppermute(value, (axis, "core"), pairs)


def swap(value, axis):
    return lax.ppermute(value, axis, [(0, 1), (1, 0)])


def turn(by):
    return by * (1 - 2 * lax.axis_index("core"))


def after(value, *others):
    return lax.optimization_barrier((value, *others))[0]


def gather(log_derivs, packed):
    z_a1, z_b1 = shift(log_derivs, "z", 1), shift(log_derivs, "z", -1)
    x_a0, x_b0 = shift(packed, "x", 1), shift(packed, "x", -1)
    partner = swap(packed, "ylo")

    z_a2, z_b2 = shift(z_a1, "z", 1), shift(z_b1, "z", -1)
    x_a1, x_far0 = shift(partner, "x", 1), shift(x_a0, "x", 1)
    x_b1 = swap(x_b0, "ylo")

    z_a3, z_b3 = shift(z_a2, "z", 1), shift(z_b2, "z", -1)
    x_far1 = shift(after(x_a1, x_far0, x_b1), "x", 1)

    z_a4 = shift(after(z_a3, z_b3), "z", 1)
    rows = {0: log_derivs, 1: z_a1, -1: z_b1, 2: z_a2, -2: z_b2, 3: z_a3, -3: z_b3, 4: z_a4}
    columns = {(0, 0): packed, (0, 1): x_a0, (0, -1): x_b0, (0, 2): x_far0}
    columns |= {(1, 0): partner, (1, 1): x_a1, (1, -1): x_b1, (1, 2): x_far1}
    return rows, columns


def pack(log_derivs, sample_vector):
    def kernel(vec, out):
        left = jnp.transpose(jnp.broadcast_to(vec[...], (ROWS, ROWS)))
        lane = lax.broadcasted_iota(jnp.int32, (ROWS, ROWS), 1)
        parts = jnp.zeros((ROWS, ROWS), F32)
        for i in range(3):
            part = left.astype(jnp.bfloat16).astype(F32)
            left = left - part
            parts = jnp.where(lane == i, part, parts)
        out[...] = parts.astype(jnp.bfloat16)

    parts = pl.pallas_call(
        kernel,
        out_shape=jax.ShapeDtypeStruct((ROWS, ROWS), jnp.bfloat16),
        in_specs=[VMEM],
        out_specs=VMEM,
        compiler_params=SMALL,
        cost_estimate=takes(0),
    )(sample_vector[None])
    return jnp.concatenate([log_derivs, parts], axis=1)


def products(scale, rows, columns, other, parts, cost):
    n = len(rows)

    def kernel(*refs):
        cols, outs, (held, sems) = refs[n : n + len(columns)], refs[n + len(columns) : -2], refs[-2:]
        copies = []
        for i, (ref, (ylo, back)) in enumerate(zip(cols, columns)):
            x = lax.rem(lax.axis_index("x") + NX - turn(back), NX)
            core = lax.rem(lax.div(x, 2) + lax.axis_index("core"), 2)
            yhi = lax.rem(lax.axis_index("ylo") + ylo + lax.axis_index("yhi"), 2)
            to = pl.multiple_of(lax.rem(x, 2) * ROWS, ROWS)
            copy = pltpu.make_async_copy(
                ref.at[:, pl.ds(0, PANEL)], held.at[yhi, pl.ds(to, ref.shape[0])], sems.at[i]
            )
            copies.append((core == other, copy))
        for mine, copy in copies:
            pl.when(mine)(copy.start)
        for mine, copy in copies:
            pl.when(mine)(copy.wait)
        block = jnp.concatenate([r[...] for r in refs[:n]], axis=0)
        for pair in range(2):
            value = scale * lax.dot_general(
                block, held[pair], (((1,), (1,)), ((), ())), preferred_element_type=F32
            )
            first = 0
            for out in outs:
                out[:, 256 * pair : 256 * pair + 256] = value[first : first + out.shape[0]]
                first += out.shape[0]

    return pl.pallas_call(
        kernel,
        out_shape=[jax.ShapeDtypeStruct((count, 512), F32) for count in parts],
        in_specs=[VMEM] * n + [ANYWHERE] * len(columns),
        out_specs=[VMEM] * len(parts),
        scratch_shapes=[
            pltpu.VMEM((2, 256, PANEL), jnp.bfloat16),
            pltpu.SemaphoreType.DMA((len(columns),)),
        ],
        compiler_params=pltpu.CompilerParams(vmem_limit_bytes=24 * 2**20),
        cost_estimate=takes(cost),
    )(*rows, *columns.values())


def term(scale, columns):
    def kernel(*refs):
        cols = refs[: len(columns)]
        out, held, vecs, sems = refs[len(columns) :]
        u = lax.axis_index("ylo") * NX + lax.axis_index("x")
        mine = pl.multiple_of(u * 256, 256)
        copies, to = [], 0
        for i, ref in enumerate(cols):
            for j, (part, target) in enumerate(((pl.ds(mine, 256), held), (pl.ds(PANEL, ROWS), vecs))):
                copy = pltpu.make_async_copy(
                    ref.at[:, part], target.at[pl.ds(to, ref.shape[0])], sems.at[2 * i + j]
                )
                copy.start()
                copies.append(copy)
            to += ref.shape[0]
        for copy in copies:
            copy.wait()
        parts = lax.dot_general(
            vecs[...], held[...], (((0,), (0,)), ((), ())), preferred_element_type=F32
        )
        out[...] = jnp.broadcast_to(scale * jnp.sum(parts, axis=0, keepdims=True), (8, 256))

    return pl.pallas_call(
        kernel,
        out_shape=jax.ShapeDtypeStruct((8, 256), F32),
        in_specs=[ANYWHERE] * len(columns),
        out_specs=VMEM,
        scratch_shapes=[
            pltpu.VMEM((8 * ROWS, 256), jnp.bfloat16),
            pltpu.VMEM((8 * ROWS, ROWS), jnp.bfloat16),
            pltpu.SemaphoreType.DMA((2 * len(columns),)),
        ],
        compiler_params=SMALL,
        cost_estimate=pl.CostEstimate(flops=2**26, bytes_accessed=2**20, transcendentals=0),
    )(*columns.values())


def peak(value):
    top = jnp.maximum(jnp.max(jnp.abs(value)), 1e-30)
    return jnp.broadcast_to(top, (16, 256)).astype(jnp.bfloat16)


def encode(value, top):
    size = jnp.log2(jnp.maximum(jnp.abs(value) * (1.0 / top.astype(F32)[:1]), 2.0**-26))
    power = jnp.exp2(jnp.maximum(126.0 + 22.0 * size, 5.0 * size - 10.0))
    return jnp.where(value < 0, -power, power).astype(jnp.bfloat16)


def decode(code, top):
    code = code.astype(F32)
    size = jnp.log2(jnp.maximum(jnp.abs(code), 2.0**-126))
    value = jnp.exp2(jnp.minimum((size - 126.0) * (1.0 / 22.0), (size + 10.0) * 0.2)) * top.astype(F32)[:1]
    return jnp.where(code < 0, -value, jnp.where(code > 0, value, 0.0))


def split_yhi(keep, received, backs, cost):
    m = keep.shape[0]
    order = [backs.index(-back if -back in backs else back) for back in backs]

    def kernel(a, *refs):
        own, code = refs[len(received) :]
        b = jnp.concatenate([ref[...] for ref in refs[: len(received)]], axis=0)
        b = jnp.concatenate([b[ROWS * i : ROWS * (i + 1)] for i in order], axis=0)
        own[...] = a[:, :256] + b[:, :256]
        other = a[:, 256:] + b[:, 256:]
        top = peak(other)
        code[:m] = encode(other, top)
        code[m:] = top

    return pl.pallas_call(
        kernel,
        out_shape=(
            jax.ShapeDtypeStruct((m, 256), F32),
            jax.ShapeDtypeStruct((m + 16, 256), jnp.bfloat16),
        ),
        in_specs=[VMEM] * (1 + len(received)),
        out_specs=(VMEM, VMEM),
        compiler_params=SMALL,
        cost_estimate=takes(cost),
    )(keep, *received)


def split_z(own, received, last_rows, backs, cost):
    m = own.shape[0]

    def kernel(own, code, rows, *outs):
        full = own[...] + decode(code[:m], code[m:])
        left, parts = rows[:1], []
        for _ in range(3):
            parts.append(left.astype(jnp.bfloat16).astype(F32))
            left = left - parts[-1]
        row = lax.broadcasted_iota(jnp.int32, (16, 256), 0)
        for i, (back, out) in enumerate(zip(backs, outs)):
            block = full[ROWS * i : ROWS * (i + 1)]
            if back == 0:
                out[...] = block
                continue
            top = peak(block)
            out[:ROWS] = encode(block, top)
            tail = jnp.where(row == 0, top.astype(F32), 0.0)
            for j in range(3):
                tail = jnp.where(row == j + 1, parts[j], tail)
            out[ROWS:] = tail.astype(jnp.bfloat16)

    whole = jax.ShapeDtypeStruct((ROWS, 256), F32)
    coded = jax.ShapeDtypeStruct((ROWS + 16, 256), jnp.bfloat16)
    return pl.pallas_call(
        kernel,
        out_shape=tuple(coded if back else whole for back in backs),
        in_specs=[VMEM] * 3,
        out_specs=tuple(VMEM for _ in backs),
        compiler_params=SMALL,
        cost_estimate=takes(cost),
    )(own, received, last_rows)


def place(blocks, total, gram, last, cost):
    n, held = len(blocks), [] if gram is None else [gram]

    def kernel(*refs):
        out, result, stage, sems = refs[n + 1 + len(held) :]
        sum_of = refs[n][:1]
        copies = []
        for i, (block, back) in enumerate(zip(refs, blocks)):
            z = lax.rem(lax.axis_index("z") + NZ + turn(back), NZ)
            at = pl.multiple_of(z * ROWS, ROWS)
            if back:
                tail = block[ROWS:]
                stage[i] = decode(block[:ROWS], tail)
                sum_of = sum_of + jnp.sum(tail[1:4].astype(F32), axis=0, keepdims=True)
            else:
                stage[i] = block[...]
            for odd in range(2):
                copy = pltpu.make_async_copy(
                    stage.at[i, :, pl.ds(odd * ROWS, ROWS)],
                    out.at[:, pl.ds(at + odd * NZ * ROWS, ROWS)],
                    sems.at[i, odd],
                )
                copy.start()
                copies.append(copy)
        if last:
            turned = pltpu.roll(jnp.broadcast_to(sum_of, (8, 256)), lax.rem(256 - 32 * lax.axis_index("z"), 256), 1)
            result[...] = turned[:1, :32]
        else:
            result[...] = jnp.broadcast_to(sum_of, (8, 256))
        for copy in copies:
            copy.wait()

    return pl.pallas_call(
        kernel,
        out_shape=(
            jax.ShapeDtypeStruct((ROWS, PANEL), F32),
            jax.ShapeDtypeStruct((1, 32) if last else (8, 256), F32),
        ),
        in_specs=[VMEM] * (n + 1) + [ANYWHERE] * len(held),
        out_specs=(ANYWHERE, VMEM),
        scratch_shapes=[pltpu.VMEM((n, ROWS, 256), F32), pltpu.SemaphoreType.DMA((n, 2))],
        input_output_aliases={n + 1: 0} if held else {},
        compiler_params=SMALL,
        cost_estimate=takes(cost),
    )(*blocks.values(), total, *held)


def body(log_derivs, sample_vector):
    scale_gram = 1.0 / math.sqrt(PANEL * 4)
    scale_update = 1.0 / math.sqrt(ROWS * 64)

    rows, columns = gather(log_derivs, pack(log_derivs, sample_vector))
    last_rows = term(scale_update, columns)

    blocks = {}
    for backs, parts, costs in zip(GROUPS, PARTS, COSTS):
        factors = [rows[back] for back in backs]
        sends = products(scale_gram, factors, columns, 1, parts, costs[0])
        received = [swap(send, "core") for send in sends]
        (keep,) = products(scale_gram, factors, columns, 0, (sum(parts),), costs[0])
        own, code = split_yhi(keep, received, backs, costs[1])
        done = split_z(own, swap(code, "yhi"), last_rows, backs, costs[2])
        for back, block in zip(backs, done):
            blocks[back] = shift(block, "z", -back) if back else block

    gram, total = None, last_rows
    for backs, cost in zip(GROUPS, PLACE_COSTS):
        gram, total = place({back: blocks[back] for back in backs}, total, gram, backs == GROUPS[-1], cost)
    return gram, total


def solution(mesh):
    fine = Mesh(mesh.devices.reshape(SIZES), AXES)
    samp, par = AXES[:3], AXES[3:]
    return jax.shard_map(
        body,
        mesh=fine,
        in_specs=(P(samp, par), P(samp)),
        out_specs=(P(samp, par), P(par, samp)),
        check_vma=False,
    )
```
